32 devices in a mesh: grp: 4 (over y, core), seq: 8 (over z, x).
Axes of the slice: x: 2, y: 2, z: 4, core: 2. Of those that a mesh axis runs over, the one named last changes fastest.
Arguments:
- tokens: bfloat16 [4, 1024, 1024], P('grp', 'seq'), may hold values from -40 to 40
- queries: bfloat16 [4, 1024, 512], P('grp', 'seq'), may hold values from -8 to 8
- keys: bfloat16 [4, 1024, 512], P('grp', 'seq'), may hold values from -8 to 8
- values: bfloat16 [4, 1024, 512], P('grp', 'seq'), may hold values from -6 to 6
- attn_mask: int32 [4, 8, 8], P('grp', 'seq'), may hold values from 0 to 1, as said below
- out_proj: bfloat16 [512, 1024], replicated, may hold values from -0.25 to 0.25
- norm_gain_vector: float32 [1024], replicated, may hold values from 0.5 to 1.5
- w1_packed: bfloat16 [32, 2, 128, 128], P('grp'), may hold values from -0.375 to 0.375
- w1_rows: int32 [32, 2], replicated, may hold values from 0 to 7, as said below
- w2_packed: bfloat16 [32, 2, 128, 128], P('grp'), may hold values from -0.1875 to 0.1875
- w2_cols: int32 [32, 2], replicated, may hold values from 0 to 7, as said below
- grad_out: bfloat16 [4, 1024, 1024], P('grp', 'seq'), may hold values from -6 to 6
Outputs:
- output: bfloat16 [4, 1024, 1024], P('grp', 'seq')
- grad_tokens: bfloat16 [4, 1024, 1024], P('grp', 'seq')
The draws below stay inside these ranges and needn't reach their ends.
Inputs may be any that keep to these rules, and one draw needn't show every extreme that they name: attn_mask[s, i, i] is 1 for every sheet s and block i. `w1_rows`: the 2 entries of a row are distinct. `w2_cols`: the 2 entries of a row are distinct.
All inputs are finite; a program needn't handle non-finite values.
Results may differ from the reference program's by a relative error of at most 0.0035.
The reference program's roundings to bfloat16 on the way count: a program that leaves them out, or rounds other values in their place, can miss the bound.
Values may be sent and summed in bfloat16 or wider, within the bound.
No kernel may reach another device: no remote copies, remote signals or barrier semaphores. Data moves between devices by JAX's collectives and lax.ppermute only.
A program may use at most 64 MiB of HBM per device.

```python
import jax
import jax.numpy as jnp
from jax import lax

D = 1024
FF = 4096
HD = 64
HEADS = 8
BLK = 128
NNZ = 2
SHEETS = 4
SEQ = 1024
NBK = 8
FB = 32
DB = 8


def scales_of(key, count):
    return 10.0 ** jax.random.uniform(key, (count,), jnp.float32, -0.5, 0.5)


def draw_tokens(key, part):
    row_scale = scales_of(jax.random.fold_in(key, 21), SHEETS * SEQ).reshape(SHEETS, SEQ, 1)
    col_scale = scales_of(jax.random.fold_in(key, 22), D)
    base = jnp.clip(jax.random.normal(jax.random.fold_in(key, 24), (SHEETS, SEQ, D), jnp.float32), -4.0, 4.0)
    return (base * row_scale * col_scale).astype(jnp.bfloat16)


def draw_queries(key, part):
    shape = (SHEETS, SEQ, HEADS * HD)
    base = jnp.clip(jax.random.normal(jax.random.fold_in(key, 42), shape, jnp.float32), -6.0, 6.0)
    return base.astype(jnp.bfloat16)


def draw_keys(key, part):
    shape = (SHEETS, SEQ, HEADS * HD)
    base = jnp.clip(jax.random.normal(jax.random.fold_in(key, 52), shape, jnp.float32), -6.0, 6.0)
    return base.astype(jnp.bfloat16)


def draw_attn_mask(key, part):
    bits = jax.random.randint(jax.random.fold_in(key, 61), (SHEETS, NBK, NBK), 0, 2)
    diagonal = (jnp.arange(NBK)[:, None] == jnp.arange(NBK)[None, :]).astype(jnp.int32)
    return jnp.maximum(bits, diagonal[None]).astype(jnp.int32)


def distinct_blocks(key):
    scores = jax.random.randint(key, (FB, DB), 0, 1048576) * DB + jnp.arange(DB)[None, :]
    order = jnp.argsort(scores, axis=1, stable=True)
    return order[:, :NNZ].astype(jnp.int32)


def draw_w1_rows(key, part):
    return distinct_blocks(jax.random.fold_in(key, 71))


def draw_w2_cols(key, part):
    return distinct_blocks(jax.random.fold_in(key, 72))


def levels(stream_key, dims, cuts, low, largest):
    factor_of, own = 1.0, jax.random.fold_in(stream_key, 6)
    for dim, blocks in cuts:
        draws = jnp.exp(jax.random.uniform(jax.random.fold_in(own, dim), (blocks,), jnp.float32, low / len(cuts), largest / len(cuts)))
        factor_of = factor_of * jnp.repeat(draws, dims[dim] // blocks).reshape([-1 if axis == dim else 1 for axis in range(len(dims))])
    return factor_of


def normal_values(own_key, extent, deviation, limit, split=(), kind=jnp.bfloat16):
    gain = levels(own_key, extent, split, -0.22, 0.18) if split else 1.0
    values = jax.random.normal(own_key, extent, jnp.float32) * deviation * gain
    return jnp.minimum(jnp.maximum(values, -limit), limit).astype(kind)


def setup_inputs(seed: int = 0) -> dict:
    key_list = jax.random.split(jax.random.key(seed), 13)
    return {
        "tokens": draw_tokens(jax.random.fold_in(key_list[12], 71), 0),
        "queries": draw_queries(jax.random.fold_in(key_list[12], 71), 0),
        "keys": draw_keys(jax.random.fold_in(key_list[12], 71), 0),
        "values": normal_values(key_list[3], (SHEETS, SEQ, HEADS * HD), 1.0, 6.0, ((0, 4), (1, 8))),
        "attn_mask": draw_attn_mask(jax.random.fold_in(key_list[12], 71), 0),
        "out_proj": normal_values(key_list[5], (HEADS * HD, D), (HEADS * HD) ** -0.5, 0.25),
        "norm_gain_vector": jnp.clip(1.0 + 0.1 * jax.random.normal(key_list[6], (D,), jnp.float32), 0.5, 1.5),
        "w1_packed": normal_values(key_list[7], (FB, NNZ, BLK, BLK), (NNZ * BLK) ** -0.5, 0.375, ((0, 4),)),
        "w1_rows": draw_w1_rows(jax.random.fold_in(key_list[12], 71), 0),
        "w2_packed": normal_values(key_list[9], (FB, NNZ, BLK, BLK), (FF * NNZ // DB) ** -0.5, 0.1875, ((0, 4),)),
        "w2_cols": draw_w2_cols(jax.random.fold_in(key_list[12], 71), 0),
        "grad_out": normal_values(key_list[11], (SHEETS, SEQ, D), 1.0, 6.0, ((0, 4), (1, 8))),
    }


def gelu_slope(pre):
    return 0.5 * (1.0 + jax.scipy.special.erf(pre * 0.7071067811865476)) + pre * jnp.exp(-0.5 * pre * pre) * 0.3989422804014327

def expand_mask(mask):
    rows_blk, cols_blk = mask.shape
    wide = jnp.broadcast_to(mask[:, None, :, None], (rows_blk, BLK, cols_blk, BLK))
    return wide.reshape(rows_blk * BLK, cols_blk * BLK) > 0

def split_heads(array):
    return array.reshape(array.shape[0], HEADS, HD).transpose(1, 0, 2)

def join_heads(array):
    return array.transpose(1, 0, 2).reshape(array.shape[1], HEADS * HD)

def attend_forward(query, key_rows, value_rows, allowed):
    scale = HD ** (-0.5)

    def one_head(args):
        q_head, k_head, v_head = args
        scores = jnp.dot(q_head, k_head.T, preferred_element_type=jnp.float32) * scale
        scores = jnp.where(allowed, scores, -jnp.inf)
        top = lax.optimization_barrier(jnp.max(scores, axis=1, keepdims=True))
        weight = jnp.exp(scores - top)
        total = lax.optimization_barrier(jnp.sum(weight, axis=1, keepdims=True))
        prob = (weight / total).astype(jnp.bfloat16)
        return jnp.dot(prob, v_head, preferred_element_type=jnp.float32)
    heads_out = lax.map(one_head, (split_heads(query), split_heads(key_rows), split_heads(value_rows)))
    return join_heads(heads_out).astype(jnp.bfloat16)

def layer_norm_forward(hidden_state, gain_vector):
    mean_row = lax.optimization_barrier(jnp.mean(hidden_state, axis=1, keepdims=True))
    mean_removed = hidden_state - mean_row
    reciprocal_deviation = lax.rsqrt(lax.optimization_barrier(jnp.mean(mean_removed * mean_removed, axis=1, keepdims=True)) + 1e-06)
    unit_rows = mean_removed * reciprocal_deviation
    return (unit_rows, reciprocal_deviation, (unit_rows * gain_vector).astype(jnp.bfloat16))

def layer_norm_backward(normed_gradient, gain_vector, unit_rows, reciprocal_deviation, gradient_rows):
    unit_gradient = normed_gradient * gain_vector
    inner_product = unit_gradient - lax.optimization_barrier(jnp.mean(unit_gradient, axis=1, keepdims=True)) - unit_rows * lax.optimization_barrier(jnp.mean(unit_gradient * unit_rows, axis=1, keepdims=True))
    return (gradient_rows.astype(jnp.float32) + reciprocal_deviation * inner_product).astype(jnp.bfloat16)

def dense_first(w1_packed, w1_rows):
    blocks = FF // BLK
    col_index = jnp.arange(blocks, dtype=jnp.int32)[:, None]
    full = jnp.zeros((D // BLK, BLK, blocks, BLK), w1_packed.dtype)
    full = full.at[w1_rows, :, col_index, :].set(w1_packed)
    return full.reshape(D, FF)

def dense_second(w2_packed, w2_cols):
    blocks = FF // BLK
    row_index = jnp.arange(blocks, dtype=jnp.int32)[:, None]
    full = jnp.zeros((blocks, BLK, D // BLK, BLK), w2_packed.dtype)
    full = full.at[row_index, :, w2_cols, :].set(w2_packed)
    return full.reshape(FF, D)

def reference(tokens, queries, keys, values, attn_mask, out_proj, norm_gain_vector, w1_packed, w1_rows, w2_packed, w2_cols, grad_out):
    first = dense_first(w1_packed, w1_rows)
    second = dense_second(w2_packed, w2_cols)

    def one_sheet(args):
        rows_in, query, key_rows, value_rows, mask, gradient_rows = args
        allowed = expand_mask(mask)
        attn = attend_forward(query, key_rows, value_rows, allowed)
        hidden_state = rows_in.astype(jnp.float32) + jnp.dot(attn, out_proj, preferred_element_type=jnp.float32)
        unit_rows, reciprocal_deviation, normed_rows = layer_norm_forward(hidden_state, norm_gain_vector)
        pre = jnp.dot(normed_rows, first, preferred_element_type=jnp.float32)
        act = jax.nn.gelu(pre, approximate=False).astype(jnp.bfloat16)
        mlp = jnp.dot(act, second, preferred_element_type=jnp.float32)
        result = (hidden_state + mlp).astype(jnp.bfloat16)
        dact = jnp.dot(gradient_rows, second.T, preferred_element_type=jnp.float32)
        dpre = (dact * gelu_slope(pre)).astype(jnp.bfloat16)
        normed_gradient = jnp.dot(dpre, first.T, preferred_element_type=jnp.float32)
        incoming_gradient_rows = layer_norm_backward(normed_gradient, norm_gain_vector, unit_rows, reciprocal_deviation, gradient_rows)
        return (result, incoming_gradient_rows)
    output, grad_tokens = lax.map(one_sheet, (tokens, queries, keys, values, attn_mask, grad_out))
    return (output, grad_tokens)
```

```python
import functools

import jax
import jax.numpy as jnp
from jax import lax
from jax.experimental import pallas as pl
from jax.experimental.pallas import tpu as pltpu
from jax.sharding import PartitionSpec as P

HD = 64
BLK = 128
NNZ = 2
LANES = 128
QUADS = 4
HEAD_BIT = 2
NT = (((1,), (1,)), ((), ()))
VMEM_LIMIT = 24 * 1024 * 1024
PACK_LIMIT = 59 * 1024 * 1024


def vmem():
    return pl.BlockSpec(memory_space=pltpu.VMEM)


def smem():
    return pl.BlockSpec(memory_space=pltpu.SMEM)


def hbm():
    return pl.BlockSpec(memory_space=pltpu.HBM)


def flips_of(seq_size):
    flips = [0]
    bit = 1
    while bit < seq_size:
        if bit not in (HEAD_BIT, 2 * HEAD_BIT):
            flips = flips + [f ^ bit for f in flips]
        bit *= 2
    return flips


def exchange(x, axis, size, flip):
    return lax.ppermute(x, axis, [(i, i ^ flip) for i in range(size)])


def after(x, *earlier):
    return lax.optimization_barrier((x, *earlier))[0]


def butterfly(x, axis, size, bits):
    held = [x]
    for bit in bits:
        held = held + [exchange(part, axis, size, bit) for part in held]
    return held


def mask_rows(seq_size):
    return 16 * ((seq_size + 15) // 16)


def pack_kernel(seq_size, q_ref, k_ref, v_ref, mask_ref, w1_ref, w2_ref, *outs):
    outs, joined_ref, sems = outs[:QUADS], outs[QUADS], outs[QUADS + 1]
    me = lax.axis_index("seq")
    group = lax.rem(me // HEAD_BIT, QUADS)
    rows = mask_rows(seq_size)
    half = w1_ref.shape[0]
    copies = []

    def start(source, target):
        copies.append(pltpu.make_async_copy(source, target, sems.at[len(copies)]))
        copies[-1].start()

    for s in range(QUADS):
        cols = pl.ds(pl.multiple_of(lax.bitwise_xor(group, s) * LANES, LANES), LANES)
        for i, ref in enumerate((q_ref, k_ref, v_ref)):
            start(ref.at[0, :, cols], outs[s].at[pl.ds(i * BLK, BLK)])
    start(w1_ref, joined_ref.at[pl.ds(0, half)])
    start(w2_ref, joined_ref.at[pl.ds(half, half)])
    row_id = lax.broadcasted_iota(jnp.int32, (rows, LANES), 0)
    for s in range(QUADS):
        there = lax.bitwise_xor(me, s * HEAD_BIT)
        allowed = jnp.zeros((rows, LANES), jnp.float32)
        for t, flip in enumerate(flips_of(seq_size)):
            for u in range(QUADS):
                block = lax.bitwise_xor(there, flip ^ (u * HEAD_BIT))
                bit = mask_ref[0, 0, block].astype(jnp.float32)
                allowed = jnp.where(row_id == t * QUADS + u, bit, allowed)
        outs[s][3 * BLK :, :] = allowed.astype(jnp.bfloat16)
    for copy in copies:
        copy.wait()


def pack(query, key, value, attn_mask, w1_packed, w2_packed, seq_size):
    rows = 3 * BLK + mask_rows(seq_size)
    joined = (2 * w1_packed.shape[0], *w1_packed.shape[1:])
    outs = pl.pallas_call(
        functools.partial(pack_kernel, seq_size),
        out_shape=[jax.ShapeDtypeStruct((rows, LANES), jnp.bfloat16)] * QUADS
        + [jax.ShapeDtypeStruct(joined, jnp.bfloat16)],
        in_specs=[hbm(), hbm(), hbm(), smem(), hbm(), hbm()],
        out_specs=[vmem()] * (QUADS + 1),
        scratch_shapes=[pltpu.SemaphoreType.DMA((3 * QUADS + 2,))],
        compiler_params=pltpu.CompilerParams(vmem_limit_bytes=PACK_LIMIT),
        name="pack",
    )(query, key, value, attn_mask, w1_packed, w2_packed)
    return outs[:QUADS], outs[QUADS]


def attend_kernel(first, last, parts, *refs):
    q_refs, refs = refs[:QUADS], refs[QUADS:]
    if not first:
        kv_refs, refs = refs[: QUADS * parts], refs[QUADS * parts :]
        state_refs, refs = refs[:3], refs[3:]
    scale = HD**-0.5 * 1.4426950408889634
    first_head = lax.broadcasted_iota(jnp.int32, (BLK, LANES), 1) < HD
    for s in range(QUADS):
        q = q_refs[s][0:BLK, :]
        zero = jnp.zeros_like(q)
        both = jnp.concatenate(
            [jnp.where(first_head, q, zero), jnp.where(first_head, zero, q)], axis=0
        )
        allowed = q_refs[s][3 * BLK :, :].astype(jnp.float32)
        if first:
            pairs = [(q_refs[u][BLK : 2 * BLK, :], q_refs[u][2 * BLK : 3 * BLK, :]) for u in range(QUADS)]
            base = 0
        else:
            pairs = [(ref[0:BLK, :], ref[BLK : 2 * BLK, :]) for ref in kv_refs]
            base = QUADS
        scores = []
        for row, (key, _) in enumerate(pairs):
            dots = lax.dot_general(both, key, NT, preferred_element_type=jnp.float32)
            scores.append(jnp.where(allowed[base + row : base + row + 1, :] > 0, dots, -1e30))
        top = functools.reduce(jnp.maximum, scores)
        if not first:
            top = jnp.maximum(top, state_refs[0][s])
        top = jnp.max(top, axis=1, keepdims=True)
        if first:
            total = jnp.zeros((2 * BLK, LANES), jnp.float32)
            mixed = jnp.zeros((2 * BLK, LANES), jnp.float32)
        else:
            shrink = jnp.exp2((state_refs[0][s] - top) * scale)
            total = state_refs[1][s] * shrink
            mixed = state_refs[2][s] * shrink
        for score, (_, value) in zip(scores, pairs):
            weight = jnp.exp2((score - top) * scale)
            total = total + weight
            mixed = mixed + jnp.dot(
                weight.astype(jnp.bfloat16), value, preferred_element_type=jnp.float32
            )
        if last:
            mixed = mixed / jnp.sum(total, axis=1, keepdims=True)
            refs[s][...] = jnp.where(first_head, mixed[:BLK], mixed[BLK:]).astype(jnp.bfloat16)
        else:
            refs[0][s] = jnp.broadcast_to(top, (2 * BLK, LANES))
            refs[1][s] = total
            refs[2][s] = mixed


def attend_own(packed):
    return pl.pallas_call(
        functools.partial(attend_kernel, True, False, 1),
        out_shape=[jax.ShapeDtypeStruct((QUADS, 2 * BLK, LANES), jnp.float32)] * 3,
        in_specs=[vmem()] * QUADS,
        out_specs=[vmem()] * 3,
        compiler_params=pltpu.CompilerParams(vmem_limit_bytes=VMEM_LIMIT),
        name="attend_own",
    )(*packed)


def attend_rest(packed, rest, state):
    return pl.pallas_call(
        functools.partial(attend_kernel, False, True, len(rest) // QUADS),
        out_shape=[jax.ShapeDtypeStruct((BLK, LANES), jnp.bfloat16)] * QUADS,
        in_specs=[vmem()] * (QUADS + len(rest) + 3),
        out_specs=[vmem()] * QUADS,
        compiler_params=pltpu.CompilerParams(vmem_limit_bytes=VMEM_LIMIT),
        name="attend_rest",
    )(*packed, *rest, *state)


def block_of(index):
    return pl.ds(pl.multiple_of(index * BLK, BLK), BLK)


def mlp_kernel(owners, rows_ref, cols_ref, *refs):
    attn_refs, refs = refs[:QUADS], refs[QUADS:]
    proj_ref, tokens_ref, gain_ref, grad_ref = refs[:4]
    weight_refs, refs = refs[4 : 4 + owners], refs[4 + owners :]
    out_ref, grad_out_ref, normed_ref, mlp_ref, back_ref, act_ref, dpre_ref, held_ref, sems = refs
    copies = [
        pltpu.make_async_copy(weight_refs[s], held_ref.at[s], sems.at[s]) for s in range(owners)
    ]
    for copy in copies:
        copy.start()
    blocks = held_ref.shape[1] // 2
    group = lax.rem(lax.axis_index("seq") // HEAD_BIT, QUADS)
    hidden = tokens_ref[0].astype(jnp.float32)
    for s in range(QUADS):
        hidden = hidden + jnp.dot(
            attn_refs[s][...],
            proj_ref[block_of(lax.bitwise_xor(group, s)), :],
            preferred_element_type=jnp.float32,
        )
    gain = gain_ref[...]
    mean = jnp.mean(hidden, axis=1, keepdims=True)
    centred = hidden - mean
    rstd = lax.rsqrt(jnp.mean(centred * centred, axis=1, keepdims=True) + 1e-06)
    unit = centred * rstd
    normed_ref[...] = (unit * gain).astype(jnp.bfloat16)
    mlp_ref[...] = hidden
    back_ref[...] = jnp.zeros_like(back_ref)
    me = lax.axis_index("grp")
    steps = [(s, c) for s in range(owners) for c in range(blocks)]

    def places(table_ref, s, c):
        block = lax.bitwise_xor(me, s) * blocks + c
        return [block_of(table_ref[n, block]) for n in range(NNZ)]

    for i, (s, c) in enumerate(steps):
        if c == 0:
            copies[s].wait()
        picked = jnp.concatenate([normed_ref[:, r] for r in places(rows_ref, s, c)], axis=1)
        grads = jnp.concatenate([grad_ref[0, :, r] for r in places(cols_ref, s, c)], axis=1)
        first = held_ref[s, c].reshape(NNZ * BLK, BLK)
        second = jnp.concatenate([held_ref[s, blocks + c, n] for n in range(NNZ)], axis=1)
        pre = jnp.dot(picked, first, preferred_element_type=jnp.float32)
        dact = lax.dot_general(grads, second, NT, preferred_element_type=jnp.float32)
        cdf = 0.5 * (1.0 + lax.erf(pre * 0.7071067811865476))
        slope = cdf + pre * jnp.exp(-0.5 * pre * pre) * 0.3989422804014327
        act_ref[i] = (pre * cdf).astype(jnp.bfloat16)
        dpre_ref[i] = (dact * slope).astype(jnp.bfloat16)
    for i, (s, c) in enumerate(steps):
        first = held_ref[s, c].reshape(NNZ * BLK, BLK)
        second = jnp.concatenate([held_ref[s, blocks + c, n] for n in range(NNZ)], axis=1)
        forward = jnp.dot(act_ref[i], second, preferred_element_type=jnp.float32)
        backward = lax.dot_general(dpre_ref[i], first, NT, preferred_element_type=jnp.float32)
        for n, col in enumerate(places(cols_ref, s, c)):
            mlp_ref[:, col] += forward[:, n * BLK : (n + 1) * BLK]
        for n, row in enumerate(places(rows_ref, s, c)):
            back_ref[:, row] += backward[:, n * BLK : (n + 1) * BLK]
    out_ref[0] = mlp_ref[...].astype(jnp.bfloat16)
    dxhat = back_ref[...] * gain
    dhidden = (
        dxhat
        - jnp.mean(dxhat, axis=1, keepdims=True)
        - unit * jnp.mean(dxhat * unit, axis=1, keepdims=True)
    )
    grad_out_ref[0] = (grad_ref[0].astype(jnp.float32) + rstd * dhidden).astype(jnp.bfloat16)


def mlp(w1_rows, w2_cols, attn, out_proj, tokens, gain, grad_out, weights):
    owners = len(weights)
    shape = tokens.shape
    hidden_blocks = w1_rows.shape[1]
    near = (*attn, out_proj, tokens, gain, grad_out)
    return pl.pallas_call(
        functools.partial(mlp_kernel, owners),
        out_shape=[jax.ShapeDtypeStruct(shape, jnp.bfloat16)] * 2,
        in_specs=[smem()] * 2 + [vmem()] * len(near) + [hbm()] * owners,
        out_specs=[vmem()] * 2,
        scratch_shapes=[
            pltpu.VMEM(shape[1:], jnp.bfloat16),
            pltpu.VMEM(shape[1:], jnp.float32),
            pltpu.VMEM(shape[1:], jnp.float32),
            pltpu.VMEM((hidden_blocks, BLK, BLK), jnp.bfloat16),
            pltpu.VMEM((hidden_blocks, BLK, BLK), jnp.bfloat16),
            pltpu.VMEM((owners, *weights[0].shape), jnp.bfloat16),
            pltpu.SemaphoreType.DMA((owners,)),
        ],
        compiler_params=pltpu.CompilerParams(vmem_limit_bytes=VMEM_LIMIT),
        name="mlp",
    )(w1_rows, w2_cols, *near, *weights)


def body(
    seq_size,
    grp_size,
    tokens,
    queries,
    keys,
    values,
    attn_mask,
    out_proj,
    norm_gain_vector,
    w1_packed,
    w1_rows,
    w2_packed,
    w2_cols,
    grad_out,
):
    grp_bits = []
    bit = grp_size // 2
    while bit:
        grp_bits.append(bit)
        bit //= 2
    flips = [f for f in flips_of(seq_size) if f and f & (f - 1) == 0]

    packed, joined = pack(queries, keys, values, attn_mask, w1_packed, w2_packed, seq_size)
    weights = {0: joined, grp_bits[0]: exchange(joined, "grp", grp_size, grp_bits[0])}
    packed = [packed[0]] + [
        exchange(packed[s], "seq", seq_size, s * HEAD_BIT) for s in range(1, QUADS)
    ]
    own = [p[BLK : 3 * BLK] for p in packed]
    held = [butterfly(part, "seq", seq_size, flips) for part in own]
    for bit in grp_bits[1:]:
        weights[bit] = exchange(after(joined, *packed[1:]), "grp", grp_size, bit)
    state = attend_own(packed)
    rest = [held[u][t] for t in range(1, len(held[0])) for u in range(QUADS)]
    attn = attend_rest(packed, rest, state)
    attn = [attn[0]] + [exchange(attn[s], "seq", seq_size, s * HEAD_BIT) for s in range(1, QUADS)]
    masks = [0]
    for bit in grp_bits:
        for m in masks:
            if m ^ bit not in weights:
                weights[m ^ bit] = exchange(after(weights[m], *attn[1:]), "grp", grp_size, bit)
        masks = masks + [m ^ bit for m in masks]
    output, grad_tokens = mlp(
        w1_rows.T,
        w2_cols.T,
        attn,
        out_proj,
        tokens,
        norm_gain_vector[None],
        grad_out,
        [weights[m] for m in range(grp_size)],
    )
    return (output, grad_tokens)


def solution(mesh):
    return jax.shard_map(
        functools.partial(body, mesh.shape["seq"], mesh.shape["grp"]),
        mesh=mesh,
        in_specs=(
            P("grp", "seq", None),
            P("grp", "seq", None),
            P("grp", "seq", None),
            P("grp", "seq", None),
            P("grp", "seq", None),
            P(),
            P(),
            P("grp", None, None, None),
            P(),
            P("grp", None, None, None),
            P(),
            P("grp", "seq", None),
        ),
        out_specs=(P("grp", "seq", None), P("grp", "seq", None)),
        check_vma=False,
    )
```

```python
import functools

import jax
import jax.numpy as jnp
from jax import lax
from jax.experimental import pallas as pl
from jax.experimental.pallas import tpu as pltpu
from jax.sharding import PartitionSpec as P

HD = 64
BLK = 128
NNZ = 2
LANES = 128
QUADS = 4
HEAD_BIT = 2
NT = (((1,), (1,)), ((), ()))
ORDER = (2, 3, 1)
VMEM_LIMIT = 24 * 1024 * 1024
PACK_LIMIT = 60 * 1024 * 1024


def vmem():
    return pl.BlockSpec(memory_space=pltpu.VMEM)


def smem():
    return pl.BlockSpec(memory_space=pltpu.SMEM)


def hbm():
    return pl.BlockSpec(memory_space=pltpu.HBM)


def flips_of(seq_size):
    flips = [0]
    bit = 1
    while bit < seq_size:
        if bit not in (HEAD_BIT, 2 * HEAD_BIT):
            flips = flips + [f ^ bit for f in flips]
        bit *= 2
    return flips


def exchange(x, axis, size, flip):
    return lax.ppermute(x, axis, [(i, i ^ flip) for i in range(size)])


def after(x, *earlier):
    return lax.optimization_barrier((x, *earlier))[0]


def butterfly(x, axis, size, bits):
    held = [x]
    for bit in bits:
        held = held + [exchange(part, axis, size, bit) for part in held]
    return held


def mask_rows(seq_size):
    return 16 * ((seq_size + 15) // 16)


def pack_kernel(seq_size, q_ref, k_ref, v_ref, mask_ref, *outs):
    me = lax.axis_index("seq")
    group = lax.rem(me // HEAD_BIT, QUADS)
    rows = mask_rows(seq_size)
    row_id = lax.broadcasted_iota(jnp.int32, (rows, LANES), 0)
    for s in range(QUADS):
        cols = pl.ds(pl.multiple_of(lax.bitwise_xor(group, s) * LANES, LANES), LANES)
        for i, ref in enumerate((q_ref, k_ref, v_ref)):
            outs[s][i * BLK : (i + 1) * BLK, :] = ref[0, :, cols]
        there = lax.bitwise_xor(me, s * HEAD_BIT)
        allowed = jnp.zeros((rows, LANES), jnp.float32)
        for t, flip in enumerate(flips_of(seq_size)):
            for u in range(QUADS):
                block = lax.bitwise_xor(there, flip ^ (u * HEAD_BIT))
                bit = mask_ref[0, 0, block].astype(jnp.float32)
                allowed = jnp.where(row_id == t * QUADS + u, bit, allowed)
        outs[s][3 * BLK :, :] = allowed.astype(jnp.bfloat16)


def pack(query, key, value, attn_mask, seq_size):
    rows = 3 * BLK + mask_rows(seq_size)
    return pl.pallas_call(
        functools.partial(pack_kernel, seq_size),
        out_shape=[jax.ShapeDtypeStruct((rows, LANES), jnp.bfloat16)] * QUADS,
        in_specs=[vmem(), vmem(), vmem(), smem()],
        out_specs=[vmem()] * QUADS,
        compiler_params=pltpu.CompilerParams(vmem_limit_bytes=PACK_LIMIT),
        name="pack",
    )(query, key, value, attn_mask)


def attend_kernel(first, last, parts, *refs):
    q_refs, refs = refs[:QUADS], refs[QUADS:]
    if first:
        rows_ref, cols_ref, gain_ref = refs[:3]
        refs = refs[3:]
        refs[3][0:NNZ, :] = rows_ref[...]
        refs[3][NNZ:, :] = cols_ref[...]
        refs[4][...] = gain_ref[...]
    else:
        kv_refs, refs = refs[: QUADS * parts], refs[QUADS * parts :]
        state_refs, refs = refs[:3], refs[3:]
    scale = HD**-0.5 * 1.4426950408889634
    first_head = lax.broadcasted_iota(jnp.int32, (BLK, LANES), 1) < HD
    for s in range(QUADS):
        q = q_refs[s][0:BLK, :]
        zero = jnp.zeros_like(q)
        both = jnp.concatenate(
            [jnp.where(first_head, q, zero), jnp.where(first_head, zero, q)], axis=0
        )
        allowed = q_refs[s][3 * BLK :, :].astype(jnp.float32)
        if first:
            pairs = [(q_refs[u][BLK : 2 * BLK, :], q_refs[u][2 * BLK : 3 * BLK, :]) for u in range(QUADS)]
            base = 0
        else:
            pairs = [(ref[0:BLK, :], ref[BLK : 2 * BLK, :]) for ref in kv_refs]
            base = QUADS
        scores = []
        for row, (key, _) in enumerate(pairs):
            dots = lax.dot_general(both, key, NT, preferred_element_type=jnp.float32)
            scores.append(jnp.where(allowed[base + row : base + row + 1, :] > 0, dots, -1e30))
        top = functools.reduce(jnp.maximum, scores)
        if not first:
            top = jnp.maximum(top, state_refs[0][s])
        top = jnp.max(top, axis=1, keepdims=True)
        if first:
            total = jnp.zeros((2 * BLK, LANES), jnp.float32)
            mixed = jnp.zeros((2 * BLK, LANES), jnp.float32)
        else:
            shrink = jnp.exp2((state_refs[0][s] - top) * scale)
            total = state_refs[1][s] * shrink
            mixed = state_refs[2][s] * shrink
        for score, (_, value) in zip(scores, pairs):
            weight = jnp.exp2((score - top) * scale)
            total = total + weight
            mixed = mixed + jnp.dot(
                weight.astype(jnp.bfloat16), value, preferred_element_type=jnp.float32
            )
        if last:
            mixed = mixed / jnp.sum(total, axis=1, keepdims=True)
            refs[s][...] = jnp.where(first_head, mixed[:BLK], mixed[BLK:]).astype(jnp.bfloat16)
        else:
            refs[0][s] = jnp.broadcast_to(top, (2 * BLK, LANES))
            refs[1][s] = total
            refs[2][s] = mixed


def attend_own(packed, w1_rows, w2_cols, gain):
    return pl.pallas_call(
        functools.partial(attend_kernel, True, False, 1),
        out_shape=[jax.ShapeDtypeStruct((QUADS, 2 * BLK, LANES), jnp.float32)] * 3
        + [
            jax.ShapeDtypeStruct((2 * NNZ, w1_rows.shape[0]), jnp.int32),
            jax.ShapeDtypeStruct((1, gain.shape[0]), jnp.float32),
        ],
        in_specs=[vmem()] * (QUADS + 3),
        out_specs=[vmem()] * 5,
        compiler_params=pltpu.CompilerParams(vmem_limit_bytes=VMEM_LIMIT),
        name="attend_own",
    )(*packed, w1_rows.T, w2_cols.T, gain[None])


def attend_rest(packed, rest, state):
    return pl.pallas_call(
        functools.partial(attend_kernel, False, True, len(rest) // QUADS),
        out_shape=[jax.ShapeDtypeStruct((BLK, LANES), jnp.bfloat16)] * QUADS,
        in_specs=[vmem()] * (QUADS + len(rest) + 3),
        out_specs=[vmem()] * QUADS,
        compiler_params=pltpu.CompilerParams(vmem_limit_bytes=VMEM_LIMIT),
        name="attend_rest",
    )(*packed, *rest, *state)


def block_of(index):
    return pl.ds(pl.multiple_of(index * BLK, BLK), BLK)


def places(table_ref, owner, blocks, i):
    block = owner * blocks + i
    return (
        [block_of(table_ref[n, block]) for n in range(NNZ)],
        [block_of(table_ref[NNZ + n, block]) for n in range(NNZ)],
    )


def tall(ref, i):
    return ref[i].reshape(NNZ * BLK, BLK)


def wide(ref, i):
    return jnp.concatenate([ref[i, n] for n in range(NNZ)], axis=1)


def slope_terms(pre):
    cdf = 0.5 * (1.0 + lax.erf(pre * 0.7071067811865476))
    return pre * cdf, cdf + pre * jnp.exp(-0.5 * pre * pre) * 0.3989422804014327


def dact_of(grad_ref, second_ref, i, cols):
    grads = jnp.concatenate([grad_ref[0, :, c] for c in cols], axis=1)
    return lax.dot_general(grads, wide(second_ref, i), NT, preferred_element_type=jnp.float32)


def hidden_blocks(table_ref, owners, first_refs, second_refs, dact, normed_ref, act_ref, dpre_ref, mlp_ref, back_ref):
    blocks = first_refs[0].shape[0]
    steps = [(s, i) for s in range(len(owners)) for i in range(blocks)]
    for k, (s, i) in enumerate(steps):
        rows, cols = places(table_ref, owners[s], blocks, i)
        picked = jnp.concatenate([normed_ref[:, r] for r in rows], axis=1)
        pre = jnp.dot(picked, tall(first_refs[s], i), preferred_element_type=jnp.float32)
        act, slope = slope_terms(pre)
        act_ref[k] = act.astype(jnp.bfloat16)
        dpre_ref[k] = (dact(k, s, i, cols) * slope).astype(jnp.bfloat16)
    for k, (s, i) in enumerate(steps):
        rows, cols = places(table_ref, owners[s], blocks, i)
        forward = jnp.dot(act_ref[k], wide(second_refs[s], i), preferred_element_type=jnp.float32)
        backward = lax.dot_general(
            dpre_ref[k], tall(first_refs[s], i), NT, preferred_element_type=jnp.float32
        )
        for n in range(NNZ):
            mlp_ref[:, cols[n]] += forward[:, n * BLK : (n + 1) * BLK]
        for n in range(NNZ):
            back_ref[:, rows[n]] += backward[:, n * BLK : (n + 1) * BLK]


def near_kernel(near, table_ref, *refs):
    attn_refs, refs = refs[:QUADS], refs[QUADS:]
    proj_ref, tokens_ref, gain_ref, grad_ref = refs[:4]
    first_refs, second_refs = refs[4 : 4 + near], refs[4 + near : 4 + 3 * near]
    refs = refs[4 + 3 * near :]
    mlp_ref, back_ref, unit_ref, rstd_ref, normed_ref, far_dact_ref, act_ref, dpre_ref = refs
    group = lax.rem(lax.axis_index("seq") // HEAD_BIT, QUADS)
    hidden = tokens_ref[0].astype(jnp.float32)
    for s in range(QUADS):
        hidden = hidden + jnp.dot(
            attn_refs[s][...],
            proj_ref[block_of(lax.bitwise_xor(group, s)), :],
            preferred_element_type=jnp.float32,
        )
    mean = jnp.mean(hidden, axis=1, keepdims=True)
    centred = hidden - mean
    rstd = lax.rsqrt(jnp.mean(centred * centred, axis=1, keepdims=True) + 1e-06)
    unit = centred * rstd
    unit_ref[...] = unit
    rstd_ref[...] = jnp.broadcast_to(rstd, rstd_ref.shape)
    normed_ref[...] = (unit * gain_ref[...]).astype(jnp.bfloat16)
    mlp_ref[...] = hidden
    back_ref[...] = jnp.zeros_like(back_ref)
    me = lax.axis_index("grp")
    owners = [lax.bitwise_xor(me, s) for s in range(2 * near)]
    blocks = first_refs[0].shape[0]
    hidden_blocks(
        table_ref,
        owners[:near],
        first_refs,
        second_refs[:near],
        lambda k, s, i, cols: dact_of(grad_ref, second_refs[s], i, cols),
        normed_ref,
        act_ref,
        dpre_ref,
        mlp_ref,
        back_ref,
    )
    for s in range(near):
        for i in range(blocks):
            _, cols = places(table_ref, owners[near + s], blocks, i)
            far_dact_ref[s * blocks + i] = dact_of(grad_ref, second_refs[near + s], i, cols)


def mlp_near(table, attn, out_proj, tokens, gain, grad_out, firsts, seconds):
    near = len(firsts)
    rows, width = tokens.shape[1:]
    kept = table.shape[1] // 2
    args = (*attn, out_proj, tokens, gain, grad_out, *firsts, *seconds)
    return pl.pallas_call(
        functools.partial(near_kernel, near),
        out_shape=[
            jax.ShapeDtypeStruct((rows, width), jnp.float32),
            jax.ShapeDtypeStruct((rows, width), jnp.float32),
            jax.ShapeDtypeStruct((rows, width), jnp.float32),
            jax.ShapeDtypeStruct((rows, LANES), jnp.float32),
            jax.ShapeDtypeStruct((rows, width), jnp.bfloat16),
            jax.ShapeDtypeStruct((kept, rows, BLK), jnp.float32),
        ],
        in_specs=[smem()] + [vmem()] * len(args),
        out_specs=[vmem()] * 6,
        scratch_shapes=[pltpu.VMEM((kept, rows, BLK), jnp.bfloat16)] * 2,
        compiler_params=pltpu.CompilerParams(vmem_limit_bytes=VMEM_LIMIT),
        name="mlp_near",
    )(table, *args)


def far_kernel(near, table_ref, gain_ref, grad_ref, *refs):
    mlp_in_ref, back_in_ref, unit_ref, rstd_ref, normed_ref, dact_ref = refs[:6]
    first_refs, second_refs = refs[6 : 6 + near], refs[6 + near : 6 + 2 * near]
    out_ref, grad_out_ref, mlp_ref, back_ref, act_ref, dpre_ref = refs[6 + 2 * near :]
    mlp_ref[...] = mlp_in_ref[...]
    back_ref[...] = back_in_ref[...]
    me = lax.axis_index("grp")
    hidden_blocks(
        table_ref,
        [lax.bitwise_xor(me, near + s) for s in range(near)],
        first_refs,
        second_refs,
        lambda k, s, i, cols: dact_ref[k],
        normed_ref,
        act_ref,
        dpre_ref,
        mlp_ref,
        back_ref,
    )
    out_ref[0] = mlp_ref[...].astype(jnp.bfloat16)
    dxhat = back_ref[...] * gain_ref[...]
    unit = unit_ref[...]
    dhidden = (
        dxhat
        - jnp.mean(dxhat, axis=1, keepdims=True)
        - unit * jnp.mean(dxhat * unit, axis=1, keepdims=True)
    )
    rstd = rstd_ref[:, 0:1]
    grad_out_ref[0] = (grad_ref[0].astype(jnp.float32) + rstd * dhidden).astype(jnp.bfloat16)


def mlp_far(table, gain, grad_out, state, firsts, seconds):
    near = len(firsts)
    shape = grad_out.shape
    kept = (table.shape[1] // 2, shape[1], BLK)
    args = (gain, grad_out, *state, *firsts, *seconds)
    return pl.pallas_call(
        functools.partial(far_kernel, near),
        out_shape=[jax.ShapeDtypeStruct(shape, jnp.bfloat16)] * 2,
        in_specs=[smem()] + [vmem()] * len(args),
        out_specs=[vmem()] * 2,
        scratch_shapes=[pltpu.VMEM(shape[1:], jnp.float32)] * 2
        + [pltpu.VMEM(kept, jnp.bfloat16)] * 2,
        compiler_params=pltpu.CompilerParams(vmem_limit_bytes=VMEM_LIMIT),
        name="mlp_far",
    )(table, *args)


def body(
    seq_size,
    grp_size,
    tokens,
    queries,
    keys,
    values,
    attn_mask,
    out_proj,
    norm_gain_vector,
    w1_packed,
    w1_rows,
    w2_packed,
    w2_cols,
    grad_out,
):
    flips = [f for f in flips_of(seq_size) if f and f & (f - 1) == 0]
    across = grp_size // 2
    near_bits = []
    bit = across // 2
    while bit:
        near_bits.append(bit)
        bit //= 2

    def over_seq(x, flip):
        return exchange(x, "seq", seq_size, flip)

    def over_grp(x, flip):
        return exchange(x, "grp", grp_size, flip)

    masks = [0]
    for bit in near_bits:
        masks = masks + [m ^ bit for m in masks]
    order = sorted(range(len(masks)), key=lambda i: masks[i])

    def over_near(x):
        held = butterfly(x, "grp", grp_size, near_bits)
        return [held[i] for i in order]

    far_second = over_grp(w2_packed, across)
    far_first = over_grp(w1_packed, across)
    packed = pack(queries, keys, values, attn_mask, seq_size)
    packed = {0: packed[0], **{s: over_seq(packed[s], s * HEAD_BIT) for s in ORDER}}
    packed = [packed[s] for s in range(QUADS)]
    held = [butterfly(p[BLK : 3 * BLK], "seq", seq_size, flips) for p in packed]
    near_seconds = over_near(after(w2_packed, *packed[1:]))
    near_firsts = over_near(after(w1_packed, *packed[1:]))
    *state, table, gain = attend_own(packed, w1_rows, w2_cols, norm_gain_vector)
    rest = [held[u][t] for t in range(1, len(held[0])) for u in range(QUADS)]
    far_seconds = over_near(after(far_second, state[0]))
    attn = attend_rest(packed, rest, state)
    attn = {0: attn[0], **{s: over_seq(attn[s], s * HEAD_BIT) for s in ORDER}}
    attn = [attn[s] for s in range(QUADS)]
    far_firsts = over_near(after(far_first, *attn[1:]))
    state = mlp_near(
        table, attn, out_proj, tokens, gain, grad_out, near_firsts, near_seconds + far_seconds
    )
    output, grad_tokens = mlp_far(table, gain, grad_out, state, far_firsts, far_seconds)
    return (output, grad_tokens)


def solution(mesh):
    return jax.shard_map(
        functools.partial(body, mesh.shape["seq"], mesh.shape["grp"]),
        mesh=mesh,
        in_specs=(
            P("grp", "seq", None),
            P("grp", "seq", None),
            P("grp", "seq", None),
            P("grp", "seq", None),
            P("grp", "seq", None),
            P(),
            P(),
            P("grp", None, None, None),
            P(),
            P("grp", None, None, None),
            P(),
            P("grp", "seq", None),
        ),
        out_specs=(P("grp", "seq", None), P("grp", "seq", None)),
        check_vma=False,
    )
```

```python
import functools

import jax
import jax.numpy as jnp
from jax import lax
from jax.experimental import pallas as pl
from jax.experimental.pallas import tpu as pltpu
from jax.sharding import PartitionSpec as P

HD = 64
BLK = 128
NNZ = 2
LANES = 128
QUADS = 4
HEAD_BIT = 2
NT = (((1,), (1,)), ((), ()))
ORDER = (2, 3, 1)
VMEM_LIMIT = 24 * 1024 * 1024
PACK_LIMIT = 60 * 1024 * 1024


def vmem():
    return pl.BlockSpec(memory_space=pltpu.VMEM)


def smem():
    return pl.BlockSpec(memory_space=pltpu.SMEM)


def hbm():
    return pl.BlockSpec(memory_space=pltpu.HBM)


def flips_of(seq_size):
    flips = [0]
    bit = 1
    while bit < seq_size:
        if bit not in (HEAD_BIT, 2 * HEAD_BIT):
            flips = flips + [f ^ bit for f in flips]
        bit *= 2
    return flips


def exchange(x, axis, size, flip):
    return lax.ppermute(x, axis, [(i, i ^ flip) for i in range(size)])


def after(x, *earlier):
    return lax.optimization_barrier((x, *earlier))[0]


def butterfly(x, axis, size, bits):
    held = [x]
    for bit in bits:
        held = held + [exchange(part, axis, size, bit) for part in held]
    return held


def mask_rows(seq_size):
    return 16 * ((seq_size + 15) // 16)


def pack_kernel(seq_size, q_ref, k_ref, v_ref, mask_ref, *outs):
    me = lax.axis_index("seq")
    group = lax.rem(me // HEAD_BIT, QUADS)
    rows = mask_rows(seq_size)
    row_id = lax.broadcasted_iota(jnp.int32, (rows, LANES), 0)
    for s in range(QUADS):
        cols = pl.ds(pl.multiple_of(lax.bitwise_xor(group, s) * LANES, LANES), LANES)
        for i, ref in enumerate((q_ref, k_ref, v_ref)):
            outs[s][i * BLK : (i + 1) * BLK, :] = ref[0, :, cols]
        there = lax.bitwise_xor(me, s * HEAD_BIT)
        allowed = jnp.zeros((rows, LANES), jnp.float32)
        for t, flip in enumerate(flips_of(seq_size)):
            for u in range(QUADS):
                block = lax.bitwise_xor(there, flip ^ (u * HEAD_BIT))
                bit = mask_ref[0, 0, block].astype(jnp.float32)
                allowed = jnp.where(row_id == t * QUADS + u, bit, allowed)
        outs[s][3 * BLK :, :] = allowed.astype(jnp.bfloat16)


def pack(query, key, value, attn_mask, seq_size):
    rows = 3 * BLK + mask_rows(seq_size)
    return pl.pallas_call(
        functools.partial(pack_kernel, seq_size),
        out_shape=[jax.ShapeDtypeStruct((rows, LANES), jnp.bfloat16)] * QUADS,
        in_specs=[vmem(), vmem(), vmem(), smem()],
        out_specs=[vmem()] * QUADS,
        compiler_params=pltpu.CompilerParams(vmem_limit_bytes=PACK_LIMIT),
        name="pack",
    )(query, key, value, attn_mask)


def attend_kernel(first, last, parts, *refs):
    q_refs, refs = refs[:QUADS], refs[QUADS:]
    if first:
        rows_ref, cols_ref, gain_ref = refs[:3]
        refs = refs[3:]
        refs[3][0:NNZ, :] = rows_ref[...]
        refs[3][NNZ:, :] = cols_ref[...]
        refs[4][...] = gain_ref[...]
    else:
        kv_refs, refs = refs[: QUADS * parts], refs[QUADS * parts :]
        state_refs, refs = refs[:3], refs[3:]
    scale = HD**-0.5 * 1.4426950408889634
    first_head = lax.broadcasted_iota(jnp.int32, (BLK, LANES), 1) < HD
    for s in range(QUADS):
        q = q_refs[s][0:BLK, :]
        zero = jnp.zeros_like(q)
        both = jnp.concatenate(
            [jnp.where(first_head, q, zero), jnp.where(first_head, zero, q)], axis=0
        )
        allowed = q_refs[s][3 * BLK :, :].astype(jnp.float32)
        if first:
            pairs = [(q_refs[u][BLK : 2 * BLK, :], q_refs[u][2 * BLK : 3 * BLK, :]) for u in range(QUADS)]
            base = 0
        else:
            pairs = [(ref[0:BLK, :], ref[BLK : 2 * BLK, :]) for ref in kv_refs]
            base = QUADS
        scores = []
        for row, (key, _) in enumerate(pairs):
            dots = lax.dot_general(both, key, NT, preferred_element_type=jnp.float32)
            scores.append(jnp.where(allowed[base + row : base + row + 1, :] > 0, dots, -1e30))
        top = functools.reduce(jnp.maximum, scores)
        if not first:
            top = jnp.maximum(top, state_refs[0][s])
        top = jnp.max(top, axis=1, keepdims=True)
        if first:
            total = jnp.zeros((2 * BLK, LANES), jnp.float32)
            mixed = jnp.zeros((2 * BLK, LANES), jnp.float32)
        else:
            shrink = jnp.exp2((state_refs[0][s] - top) * scale)
            total = state_refs[1][s] * shrink
            mixed = state_refs[2][s] * shrink
        for score, (_, value) in zip(scores, pairs):
            weight = jnp.exp2((score - top) * scale)
            total = total + weight
            mixed = mixed + jnp.dot(
                weight.astype(jnp.bfloat16), value, preferred_element_type=jnp.float32
            )
        if last:
            mixed = mixed / jnp.sum(total, axis=1, keepdims=True)
            refs[s][...] = jnp.where(first_head, mixed[:BLK], mixed[BLK:]).astype(jnp.bfloat16)
        else:
            refs[0][s] = jnp.broadcast_to(top, (2 * BLK, LANES))
            refs[1][s] = total
            refs[2][s] = mixed


def attend_own(packed, w1_rows, w2_cols, gain):
    return pl.pallas_call(
        functools.partial(attend_kernel, True, False, 1),
        out_shape=[jax.ShapeDtypeStruct((QUADS, 2 * BLK, LANES), jnp.float32)] * 3
        + [
            jax.ShapeDtypeStruct((2 * NNZ, w1_rows.shape[0]), jnp.int32),
            jax.ShapeDtypeStruct((1, gain.shape[0]), jnp.float32),
        ],
        in_specs=[vmem()] * (QUADS + 3),
        out_specs=[vmem()] * 5,
        compiler_params=pltpu.CompilerParams(vmem_limit_bytes=VMEM_LIMIT),
        name="attend_own",
    )(*packed, w1_rows.T, w2_cols.T, gain[None])


def attend_rest(packed, rest, state):
    return pl.pallas_call(
        functools.partial(attend_kernel, False, True, len(rest) // QUADS),
        out_shape=[jax.ShapeDtypeStruct((BLK, LANES), jnp.bfloat16)] * QUADS,
        in_specs=[vmem()] * (QUADS + len(rest) + 3),
        out_specs=[vmem()] * QUADS,
        compiler_params=pltpu.CompilerParams(vmem_limit_bytes=VMEM_LIMIT),
        name="attend_rest",
    )(*packed, *rest, *state)


def block_of(index):
    return pl.ds(pl.multiple_of(index * BLK, BLK), BLK)


def places(table_ref, owner, blocks, i):
    block = owner * blocks + i
    return (
        [block_of(table_ref[n, block]) for n in range(NNZ)],
        [block_of(table_ref[NNZ + n, block]) for n in range(NNZ)],
    )


def tall(ref, i):
    return ref[i].reshape(NNZ * BLK, BLK)


def wide(ref, i):
    return jnp.concatenate([ref[i, n] for n in range(NNZ)], axis=1)


def slope_terms(pre):
    cdf = 0.5 * (1.0 + lax.erf(pre * 0.7071067811865476))
    return pre * cdf, cdf + pre * jnp.exp(-0.5 * pre * pre) * 0.3989422804014327


def dact_of(grad_ref, second_ref, i, cols):
    grads = jnp.concatenate([grad_ref[0, :, c] for c in cols], axis=1)
    return lax.dot_general(grads, wide(second_ref, i), NT, preferred_element_type=jnp.float32)


def hidden_blocks(table_ref, owners, first_refs, second_refs, dact, normed_ref, act_ref, dpre_ref, mlp_ref, back_ref):
    blocks = first_refs[0].shape[0]
    steps = [(s, i) for s in range(len(owners)) for i in range(blocks)]
    for k, (s, i) in enumerate(steps):
        rows, cols = places(table_ref, owners[s], blocks, i)
        picked = jnp.concatenate([normed_ref[:, r] for r in rows], axis=1)
        pre = jnp.dot(picked, tall(first_refs[s], i), preferred_element_type=jnp.float32)
        act, slope = slope_terms(pre)
        act_ref[k] = act.astype(jnp.bfloat16)
        dpre_ref[k] = (dact(k, s, i, cols) * slope).astype(jnp.bfloat16)
    for k, (s, i) in enumerate(steps):
        rows, cols = places(table_ref, owners[s], blocks, i)
        forward = jnp.dot(act_ref[k], wide(second_refs[s], i), preferred_element_type=jnp.float32)
        backward = lax.dot_general(
            dpre_ref[k], tall(first_refs[s], i), NT, preferred_element_type=jnp.float32
        )
        for n in range(NNZ):
            mlp_ref[:, cols[n]] += forward[:, n * BLK : (n + 1) * BLK]
        for n in range(NNZ):
            back_ref[:, rows[n]] += backward[:, n * BLK : (n + 1) * BLK]


def near_kernel(near, table_in_ref, *refs):
    refs, (table_ref, table_sem) = refs[:-2], refs[-2:]
    table_copy = pltpu.make_async_copy(table_in_ref, table_ref, table_sem)
    table_copy.start()
    attn_refs, refs = refs[:QUADS], refs[QUADS:]
    proj_ref, tokens_ref, gain_ref, grad_ref = refs[:4]
    first_refs, second_refs = refs[4 : 4 + near], refs[4 + near : 4 + 3 * near]
    refs = refs[4 + 3 * near :]
    mlp_ref, back_ref, unit_ref, rstd_ref, normed_ref, far_dact_ref, act_ref, dpre_ref = refs
    group = lax.rem(lax.axis_index("seq") // HEAD_BIT, QUADS)
    hidden = tokens_ref[0].astype(jnp.float32)
    for s in range(QUADS):
        hidden = hidden + jnp.dot(
            attn_refs[s][...],
            proj_ref[block_of(lax.bitwise_xor(group, s)), :],
            preferred_element_type=jnp.float32,
        )
    mean = jnp.mean(hidden, axis=1, keepdims=True)
    centred = hidden - mean
    rstd = lax.rsqrt(jnp.mean(centred * centred, axis=1, keepdims=True) + 1e-06)
    unit = centred * rstd
    unit_ref[...] = unit
    rstd_ref[...] = jnp.broadcast_to(rstd, rstd_ref.shape)
    normed_ref[...] = (unit * gain_ref[...]).astype(jnp.bfloat16)
    mlp_ref[...] = hidden
    back_ref[...] = jnp.zeros_like(back_ref)
    table_copy.wait()
    me = lax.axis_index("grp")
    owners = [lax.bitwise_xor(me, s) for s in range(2 * near)]
    blocks = first_refs[0].shape[0]
    hidden_blocks(
        table_ref,
        owners[:near],
        first_refs,
        second_refs[:near],
        lambda k, s, i, cols: dact_of(grad_ref, second_refs[s], i, cols),
        normed_ref,
        act_ref,
        dpre_ref,
        mlp_ref,
        back_ref,
    )
    for s in range(near):
        for i in range(blocks):
            _, cols = places(table_ref, owners[near + s], blocks, i)
            far_dact_ref[s * blocks + i] = dact_of(grad_ref, second_refs[near + s], i, cols)


def mlp_near(table, attn, out_proj, tokens, gain, grad_out, firsts, seconds):
    near = len(firsts)
    rows, width = tokens.shape[1:]
    kept = table.shape[1] // 2
    args = (*attn, out_proj, tokens, gain, grad_out, *firsts, *seconds)
    return pl.pallas_call(
        functools.partial(near_kernel, near),
        out_shape=[
            jax.ShapeDtypeStruct((rows, width), jnp.float32),
            jax.ShapeDtypeStruct((rows, width), jnp.float32),
            jax.ShapeDtypeStruct((rows, width), jnp.float32),
            jax.ShapeDtypeStruct((rows, LANES), jnp.float32),
            jax.ShapeDtypeStruct((rows, width), jnp.bfloat16),
            jax.ShapeDtypeStruct((kept, rows, BLK), jnp.float32),
        ],
        in_specs=[vmem()] * (1 + len(args)),
        out_specs=[vmem()] * 6,
        scratch_shapes=[pltpu.VMEM((kept, rows, BLK), jnp.bfloat16)] * 2
        + [pltpu.SMEM(table.shape, jnp.int32), pltpu.SemaphoreType.DMA],
        compiler_params=pltpu.CompilerParams(vmem_limit_bytes=VMEM_LIMIT),
        name="mlp_near",
    )(table, *args)


def far_kernel(near, table_in_ref, gain_ref, grad_ref, *refs):
    refs, (table_ref, table_sem) = refs[:-2], refs[-2:]
    table_copy = pltpu.make_async_copy(table_in_ref, table_ref, table_sem)
    table_copy.start()
    mlp_in_ref, back_in_ref, unit_ref, rstd_ref, normed_ref, dact_ref = refs[:6]
    first_refs, second_refs = refs[6 : 6 + near], refs[6 + near : 6 + 2 * near]
    out_ref, grad_out_ref, mlp_ref, back_ref, act_ref, dpre_ref = refs[6 + 2 * near :]
    mlp_ref[...] = mlp_in_ref[...]
    back_ref[...] = back_in_ref[...]
    table_copy.wait()
    me = lax.axis_index("grp")
    hidden_blocks(
        table_ref,
        [lax.bitwise_xor(me, near + s) for s in range(near)],
        first_refs,
        second_refs,
        lambda k, s, i, cols: dact_ref[k],
        normed_ref,
        act_ref,
        dpre_ref,
        mlp_ref,
        back_ref,
    )
    out_ref[0] = mlp_ref[...].astype(jnp.bfloat16)
    dxhat = back_ref[...] * gain_ref[...]
    unit = unit_ref[...]
    dhidden = (
        dxhat
        - jnp.mean(dxhat, axis=1, keepdims=True)
        - unit * jnp.mean(dxhat * unit, axis=1, keepdims=True)
    )
    rstd = rstd_ref[:, 0:1]
    grad_out_ref[0] = (grad_ref[0].astype(jnp.float32) + rstd * dhidden).astype(jnp.bfloat16)


def mlp_far(table, gain, grad_out, state, firsts, seconds):
    near = len(firsts)
    shape = grad_out.shape
    kept = (table.shape[1] // 2, shape[1], BLK)
    args = (gain, grad_out, *state, *firsts, *seconds)
    return pl.pallas_call(
        functools.partial(far_kernel, near),
        out_shape=[jax.ShapeDtypeStruct(shape, jnp.bfloat16)] * 2,
        in_specs=[vmem()] * (1 + len(args)),
        out_specs=[vmem()] * 2,
        scratch_shapes=[pltpu.VMEM(shape[1:], jnp.float32)] * 2
        + [pltpu.VMEM(kept, jnp.bfloat16)] * 2
        + [pltpu.SMEM(table.shape, jnp.int32), pltpu.SemaphoreType.DMA],
        compiler_params=pltpu.CompilerParams(vmem_limit_bytes=VMEM_LIMIT),
        name="mlp_far",
    )(table, *args)


def body(
    seq_size,
    grp_size,
    tokens,
    queries,
    keys,
    values,
    attn_mask,
    out_proj,
    norm_gain_vector,
    w1_packed,
    w1_rows,
    w2_packed,
    w2_cols,
    grad_out,
):
    flips = [f for f in flips_of(seq_size) if f and f & (f - 1) == 0]
    across = grp_size // 2
    near_bits = []
    bit = across // 2
    while bit:
        near_bits.append(bit)
        bit //= 2

    def over_seq(x, flip):
        return exchange(x, "seq", seq_size, flip)

    def over_grp(x, flip):
        return exchange(x, "grp", grp_size, flip)

    masks = [0]
    for bit in near_bits:
        masks = masks + [m ^ bit for m in masks]
    order = sorted(range(len(masks)), key=lambda i: masks[i])

    def over_near(x):
        held = butterfly(x, "grp", grp_size, near_bits)
        return [held[i] for i in order]

    far_second = over_grp(w2_packed, across)
    far_first = over_grp(w1_packed, across)
    packed = pack(queries, keys, values, attn_mask, seq_size)
    packed = {0: packed[0], **{s: over_seq(packed[s], s * HEAD_BIT) for s in ORDER}}
    packed = [packed[s] for s in range(QUADS)]
    held = [butterfly(p[BLK : 3 * BLK], "seq", seq_size, flips) for p in packed]
    near_seconds = over_near(after(w2_packed, *packed[1:]))
    near_firsts = over_near(after(w1_packed, *packed[1:]))
    *state, table, gain = attend_own(packed, w1_rows, w2_cols, norm_gain_vector)
    rest = [held[u][t] for t in range(1, len(held[0])) for u in range(QUADS)]
    far_seconds = over_near(after(far_second, state[0]))
    attn = attend_rest(packed, rest, state)
    attn = {0: attn[0], **{s: over_seq(attn[s], s * HEAD_BIT) for s in ORDER}}
    attn = [attn[s] for s in range(QUADS)]
    far_firsts = over_near(after(far_first, *attn[1:]))
    state = mlp_near(
        table, attn, out_proj, tokens, gain, grad_out, near_firsts, near_seconds + far_seconds
    )
    output, grad_tokens = mlp_far(table, gain, grad_out, state, far_firsts, far_seconds)
    return (output, grad_tokens)


def solution(mesh):
    return jax.shard_map(
        functools.partial(body, mesh.shape["seq"], mesh.shape["grp"]),
        mesh=mesh,
        in_specs=(
            P("grp", "seq", None),
            P("grp", "seq", None),
            P("grp", "seq", None),
            P("grp", "seq", None),
            P("grp", "seq", None),
            P(),
            P(),
            P("grp", None, None, None),
            P(),
            P("grp", None, None, None),
            P(),
            P("grp", "seq", None),
        ),
        out_specs=(P("grp", "seq", None), P("grp", "seq", None)),
        check_vma=False,
    )
```

```python
import functools

import jax
import jax.numpy as jnp
from jax import lax
from jax.experimental import pallas as pl
from jax.experimental.pallas import tpu as pltpu
from jax.sharding import PartitionSpec as P

HD = 64
BLK = 128
NNZ = 2
LANES = 128
QUADS = 4
HEAD_BIT = 2
NT = (((1,), (1,)), ((), ()))
ORDER = (2, 3, 1)
VMEM_LIMIT = 24 * 1024 * 1024
PACK_LIMIT = 60 * 1024 * 1024


def vmem():
    return pl.BlockSpec(memory_space=pltpu.VMEM)


def smem():
    return pl.BlockSpec(memory_space=pltpu.SMEM)


def hbm():
    return pl.BlockSpec(memory_space=pltpu.HBM)


def flips_of(seq_size):
    flips = [0]
    bit = 1
    while bit < seq_size:
        if bit not in (HEAD_BIT, 2 * HEAD_BIT):
            flips = flips + [f ^ bit for f in flips]
        bit *= 2
    return flips


def exchange(x, axis, size, flip):
    return lax.ppermute(x, axis, [(i, i ^ flip) for i in range(size)])


def after(x, *earlier):
    return lax.optimization_barrier((x, *earlier))[0]


def butterfly(x, axis, size, bits):
    held = [x]
    for bit in bits:
        held = held + [exchange(part, axis, size, bit) for part in held]
    return held


def mask_rows(seq_size):
    return 16 * ((seq_size + 15) // 16)


def pack_kernel(seq_size, q_ref, k_ref, v_ref, mask_ref, *outs):
    me = lax.axis_index("seq")
    group = lax.rem(me // HEAD_BIT, QUADS)
    rows = mask_rows(seq_size)
    row_id = lax.broadcasted_iota(jnp.int32, (rows, LANES), 0)
    for s in range(QUADS):
        cols = pl.ds(pl.multiple_of(lax.bitwise_xor(group, s) * LANES, LANES), LANES)
        for i, ref in enumerate((q_ref, k_ref, v_ref)):
            outs[s][i * BLK : (i + 1) * BLK, :] = ref[0, :, cols]
        there = lax.bitwise_xor(me, s * HEAD_BIT)
        allowed = jnp.zeros((rows, LANES), jnp.float32)
        for t, flip in enumerate(flips_of(seq_size)):
            for u in range(QUADS):
                block = lax.bitwise_xor(there, flip ^ (u * HEAD_BIT))
                bit = mask_ref[0, 0, block].astype(jnp.float32)
                allowed = jnp.where(row_id == t * QUADS + u, bit, allowed)
        outs[s][3 * BLK :, :] = allowed.astype(jnp.bfloat16)


def pack(query, key, value, attn_mask, seq_size):
    rows = 3 * BLK + mask_rows(seq_size)
    return pl.pallas_call(
        functools.partial(pack_kernel, seq_size),
        out_shape=[jax.ShapeDtypeStruct((rows, LANES), jnp.bfloat16)] * QUADS,
        in_specs=[vmem(), vmem(), vmem(), smem()],
        out_specs=[vmem()] * QUADS,
        compiler_params=pltpu.CompilerParams(vmem_limit_bytes=PACK_LIMIT),
        name="pack",
    )(query, key, value, attn_mask)


def attend_kernel(first, last, parts, *refs):
    q_refs, refs = refs[:QUADS], refs[QUADS:]
    if first:
        rows_ref, cols_ref, gain_ref = refs[:3]
        refs = refs[3:]
        refs[3][0:NNZ, :] = rows_ref[...]
        refs[3][NNZ:, :] = cols_ref[...]
        refs[4][...] = gain_ref[...]
    else:
        kv_refs, refs = refs[: QUADS * parts], refs[QUADS * parts :]
        state_refs, refs = refs[:3], refs[3:]
    scale = HD**-0.5 * 1.4426950408889634
    first_head = lax.broadcasted_iota(jnp.int32, (BLK, LANES), 1) < HD
    for s in range(QUADS):
        q = q_refs[s][0:BLK, :]
        zero = jnp.zeros_like(q)
        both = jnp.concatenate(
            [jnp.where(first_head, q, zero), jnp.where(first_head, zero, q)], axis=0
        )
        allowed = q_refs[s][3 * BLK :, :].astype(jnp.float32)
        if first:
            pairs = [(q_refs[u][BLK : 2 * BLK, :], q_refs[u][2 * BLK : 3 * BLK, :]) for u in range(QUADS)]
            base = 0
        else:
            pairs = [(ref[0:BLK, :], ref[BLK : 2 * BLK, :]) for ref in kv_refs]
            base = QUADS
        scores = []
        for row, (key, _) in enumerate(pairs):
            dots = lax.dot_general(both, key, NT, preferred_element_type=jnp.float32)
            scores.append(jnp.where(allowed[base + row : base + row + 1, :] > 0, dots, -1e30))
        top = functools.reduce(jnp.maximum, scores)
        if not first:
            top = jnp.maximum(top, state_refs[0][s])
        top = jnp.max(top, axis=1, keepdims=True)
        if first:
            total = jnp.zeros((2 * BLK, LANES), jnp.float32)
            mixed = jnp.zeros((2 * BLK, LANES), jnp.float32)
        else:
            shrink = jnp.exp2((state_refs[0][s] - top) * scale)
            total = state_refs[1][s] * shrink
            mixed = state_refs[2][s] * shrink
        for score, (_, value) in zip(scores, pairs):
            weight = jnp.exp2((score - top) * scale)
            total = total + weight
            mixed = mixed + jnp.dot(
                weight.astype(jnp.bfloat16), value, preferred_element_type=jnp.float32
            )
        if last:
            mixed = mixed / jnp.sum(total, axis=1, keepdims=True)
            refs[s][...] = jnp.where(first_head, mixed[:BLK], mixed[BLK:]).astype(jnp.bfloat16)
        else:
            refs[0][s] = jnp.broadcast_to(top, (2 * BLK, LANES))
            refs[1][s] = total
            refs[2][s] = mixed


def attend_own(packed, w1_rows, w2_cols, gain):
    return pl.pallas_call(
        functools.partial(attend_kernel, True, False, 1),
        out_shape=[jax.ShapeDtypeStruct((QUADS, 2 * BLK, LANES), jnp.float32)] * 3
        + [
            jax.ShapeDtypeStruct((2 * NNZ, w1_rows.shape[0]), jnp.int32),
            jax.ShapeDtypeStruct((1, gain.shape[0]), jnp.float32),
        ],
        in_specs=[vmem()] * (QUADS + 3),
        out_specs=[vmem()] * 5,
        compiler_params=pltpu.CompilerParams(vmem_limit_bytes=VMEM_LIMIT),
        name="attend_own",
    )(*packed, w1_rows.T, w2_cols.T, gain[None])


def attend_rest(packed, rest, state):
    return pl.pallas_call(
        functools.partial(attend_kernel, False, True, len(rest) // QUADS),
        out_shape=[jax.ShapeDtypeStruct((BLK, LANES), jnp.bfloat16)] * QUADS,
        in_specs=[vmem()] * (QUADS + len(rest) + 3),
        out_specs=[vmem()] * QUADS,
        compiler_params=pltpu.CompilerParams(vmem_limit_bytes=VMEM_LIMIT),
        name="attend_rest",
    )(*packed, *rest, *state)


def block_of(index):
    return pl.ds(pl.multiple_of(index * BLK, BLK), BLK)


def places(table_ref, owner, blocks, i):
    block = owner * blocks + i
    return (
        [table_ref[n, block] for n in range(NNZ)],
        [table_ref[NNZ + n, block] for n in range(NNZ)],
    )


def split_blocks(ref, blocks_ref):
    for d in range(blocks_ref.shape[0]):
        blocks_ref[d] = ref[0, :, d * BLK : (d + 1) * BLK]


def tall(ref, i):
    return ref[i].reshape(NNZ * BLK, BLK)


def wide(ref, i):
    return jnp.concatenate([ref[i, n] for n in range(NNZ)], axis=1)


def slope_terms(pre):
    cdf = 0.5 * (1.0 + lax.erf(pre * 0.7071067811865476))
    return pre * cdf, cdf + pre * jnp.exp(-0.5 * pre * pre) * 0.3989422804014327


def dact_of(grad_ref, second_ref, i, cols):
    grads = jnp.concatenate([grad_ref[c] for c in cols], axis=1)
    return lax.dot_general(grads, wide(second_ref, i), NT, preferred_element_type=jnp.float32)


def hidden_blocks(table_ref, owners, weight_refs, grad_ref, normed_ref, act_ref, dpre_ref, mlp_ref, back_ref):
    blocks = weight_refs[0].shape[0] // 2
    steps = [(s, i) for s in range(len(owners)) for i in range(blocks)]
    for k, (s, i) in enumerate(steps):
        rows, cols = places(table_ref, owners[s], blocks, i)
        dact = dact_of(grad_ref, weight_refs[s], blocks + i, cols)
        picked = jnp.concatenate([normed_ref[r] for r in rows], axis=1)
        pre = jnp.dot(picked, tall(weight_refs[s], i), preferred_element_type=jnp.float32)
        act, slope = slope_terms(pre)
        act_ref[k] = act.astype(jnp.bfloat16)
        dpre_ref[k] = (dact * slope).astype(jnp.bfloat16)
    for k, (s, i) in enumerate(steps):
        rows, cols = places(table_ref, owners[s], blocks, i)
        forward = jnp.dot(act_ref[k], wide(weight_refs[s], blocks + i), preferred_element_type=jnp.float32)
        backward = lax.dot_general(
            dpre_ref[k], tall(weight_refs[s], i), NT, preferred_element_type=jnp.float32
        )
        for n in range(NNZ):
            mlp_ref[cols[n]] += forward[:, n * BLK : (n + 1) * BLK]
        for n in range(NNZ):
            back_ref[rows[n]] += backward[:, n * BLK : (n + 1) * BLK]


def near_kernel(near, table_in_ref, *refs):
    refs, (table_ref, table_sem) = refs[:-2], refs[-2:]
    table_copy = pltpu.make_async_copy(table_in_ref, table_ref, table_sem)
    table_copy.start()
    attn_refs, refs = refs[:QUADS], refs[QUADS:]
    proj_ref, tokens_ref, gain_ref, grad_ref = refs[:4]
    weight_refs, refs = refs[4 : 4 + near], refs[4 + near :]
    mlp_ref, back_ref, unit_ref, rstd_ref, normed_ref, act_ref, dpre_ref, grads_ref = refs
    split_blocks(grad_ref, grads_ref)
    group = lax.rem(lax.axis_index("seq") // HEAD_BIT, QUADS)
    hidden = tokens_ref[0].astype(jnp.float32)
    for s in range(QUADS):
        hidden = hidden + jnp.dot(
            attn_refs[s][...],
            proj_ref[block_of(lax.bitwise_xor(group, s)), :],
            preferred_element_type=jnp.float32,
        )
    mean = jnp.mean(hidden, axis=1, keepdims=True)
    centred = hidden - mean
    rstd = lax.rsqrt(jnp.mean(centred * centred, axis=1, keepdims=True) + 1e-06)
    unit = centred * rstd
    unit_ref[...] = unit
    rstd_ref[...] = jnp.broadcast_to(rstd, rstd_ref.shape)
    normed = (unit * gain_ref[...]).astype(jnp.bfloat16)
    for d in range(mlp_ref.shape[0]):
        normed_ref[d] = normed[:, d * BLK : (d + 1) * BLK]
        mlp_ref[d] = hidden[:, d * BLK : (d + 1) * BLK]
    back_ref[...] = jnp.zeros_like(back_ref)
    table_copy.wait()
    me = lax.axis_index("grp")
    owners = [lax.bitwise_xor(me, s) for s in range(near)]
    hidden_blocks(
        table_ref,
        owners,
        weight_refs,
        grads_ref,
        normed_ref,
        act_ref,
        dpre_ref,
        mlp_ref,
        back_ref,
    )


def mlp_near(table, attn, out_proj, tokens, gain, grad_out, weights):
    near = len(weights)
    rows, width = tokens.shape[1:]
    kept = table.shape[1] // 2
    args = (*attn, out_proj, tokens, gain, grad_out, *weights)
    return pl.pallas_call(
        functools.partial(near_kernel, near),
        out_shape=[
            jax.ShapeDtypeStruct((width // BLK, rows, BLK), jnp.float32),
            jax.ShapeDtypeStruct((width // BLK, rows, BLK), jnp.float32),
            jax.ShapeDtypeStruct((rows, width), jnp.float32),
            jax.ShapeDtypeStruct((rows, LANES), jnp.float32),
            jax.ShapeDtypeStruct((width // BLK, rows, BLK), jnp.bfloat16),
        ],
        in_specs=[vmem()] * (1 + len(args)),
        out_specs=[vmem()] * 5,
        scratch_shapes=[pltpu.VMEM((kept, rows, BLK), jnp.bfloat16)] * 2
        + [pltpu.VMEM((width // BLK, rows, BLK), jnp.bfloat16)]
        + [pltpu.SMEM(table.shape, jnp.int32), pltpu.SemaphoreType.DMA],
        compiler_params=pltpu.CompilerParams(vmem_limit_bytes=VMEM_LIMIT),
        name="mlp_near",
    )(table, *args)


def far_kernel(near, table_in_ref, gain_ref, grad_ref, *refs):
    refs, (table_ref, table_sem) = refs[:-2], refs[-2:]
    table_copy = pltpu.make_async_copy(table_in_ref, table_ref, table_sem)
    table_copy.start()
    mlp_in_ref, back_in_ref, unit_ref, rstd_ref, normed_ref = refs[:5]
    weight_refs = refs[5 : 5 + near]
    out_ref, grad_out_ref, mlp_ref, back_ref, act_ref, dpre_ref, grads_ref = refs[5 + near :]
    split_blocks(grad_ref, grads_ref)
    mlp_ref[...] = mlp_in_ref[...]
    back_ref[...] = back_in_ref[...]
    table_copy.wait()
    me = lax.axis_index("grp")
    hidden_blocks(
        table_ref,
        [lax.bitwise_xor(me, near + s) for s in range(near)],
        weight_refs,
        grads_ref,
        normed_ref,
        act_ref,
        dpre_ref,
        mlp_ref,
        back_ref,
    )
    width_blocks = range(mlp_ref.shape[0])
    for d in width_blocks:
        out_ref[0, :, d * BLK : (d + 1) * BLK] = mlp_ref[d].astype(jnp.bfloat16)
    dxhat = jnp.concatenate([back_ref[d] for d in width_blocks], axis=1) * gain_ref[...]
    unit = unit_ref[...]
    dhidden = (
        dxhat
        - jnp.mean(dxhat, axis=1, keepdims=True)
        - unit * jnp.mean(dxhat * unit, axis=1, keepdims=True)
    )
    rstd = rstd_ref[:, 0:1]
    grad_out_ref[0] = (grad_ref[0].astype(jnp.float32) + rstd * dhidden).astype(jnp.bfloat16)


def mlp_far(table, gain, grad_out, state, weights):
    near = len(weights)
    shape = grad_out.shape
    kept = (table.shape[1] // 2, shape[1], BLK)
    args = (gain, grad_out, *state, *weights)
    return pl.pallas_call(
        functools.partial(far_kernel, near),
        out_shape=[jax.ShapeDtypeStruct(shape, jnp.bfloat16)] * 2,
        in_specs=[vmem()] * (1 + len(args)),
        out_specs=[vmem()] * 2,
        scratch_shapes=[pltpu.VMEM(state[0].shape, jnp.float32)] * 2
        + [pltpu.VMEM(kept, jnp.bfloat16)] * 2
        + [pltpu.VMEM(state[4].shape, jnp.bfloat16)]
        + [pltpu.SMEM(table.shape, jnp.int32), pltpu.SemaphoreType.DMA],
        compiler_params=pltpu.CompilerParams(vmem_limit_bytes=VMEM_LIMIT),
        name="mlp_far",
    )(table, *args)


def body(
    seq_size,
    grp_size,
    tokens,
    queries,
    keys,
    values,
    attn_mask,
    out_proj,
    norm_gain_vector,
    w1_packed,
    w1_rows,
    w2_packed,
    w2_cols,
    grad_out,
):
    flips = [f for f in flips_of(seq_size) if f and f & (f - 1) == 0]
    across = grp_size // 2
    near_bits = []
    bit = across // 2
    while bit:
        near_bits.append(bit)
        bit //= 2

    def over_seq(x, flip):
        return exchange(x, "seq", seq_size, flip)

    def over_grp(x, flip):
        return exchange(x, "grp", grp_size, flip)

    masks = [0]
    for bit in near_bits:
        masks = masks + [m ^ bit for m in masks]
    order = sorted(range(len(masks)), key=lambda i: masks[i])

    def over_near(x):
        held = butterfly(x, "grp", grp_size, near_bits)
        return [held[i] for i in order]

    weights = jnp.concatenate([w1_packed, w2_packed])
    far_weights = over_grp(weights, across)
    packed = pack(queries, keys, values, attn_mask, seq_size)
    packed = {0: packed[0], **{s: over_seq(packed[s], s * HEAD_BIT) for s in ORDER}}
    packed = [packed[s] for s in range(QUADS)]
    held = [butterfly(p[BLK : 3 * BLK], "seq", seq_size, flips) for p in packed]
    near_weights = over_near(after(weights, *packed[1:]))
    *state, table, gain = attend_own(packed, w1_rows, w2_cols, norm_gain_vector)
    rest = [held[u][t] for t in range(1, len(held[0])) for u in range(QUADS)]
    attn = attend_rest(packed, rest, state)
    attn = {0: attn[0], **{s: over_seq(attn[s], s * HEAD_BIT) for s in ORDER}}
    attn = [attn[s] for s in range(QUADS)]
    far_weights = over_near(after(far_weights, *attn[1:]))
    state = mlp_near(table, attn, out_proj, tokens, gain, grad_out, near_weights)
    output, grad_tokens = mlp_far(table, gain, grad_out, state, far_weights)
    return (output, grad_tokens)


def solution(mesh):
    return jax.shard_map(
        functools.partial(body, mesh.shape["seq"], mesh.shape["grp"]),
        mesh=mesh,
        in_specs=(
            P("grp", "seq", None),
            P("grp", "seq", None),
            P("grp", "seq", None),
            P("grp", "seq", None),
            P("grp", "seq", None),
            P(),
            P(),
            P("grp", None, None, None),
            P(),
            P("grp", None, None, None),
            P(),
            P("grp", "seq", None),
        ),
        out_specs=(P("grp", "seq", None), P("grp", "seq", None)),
        check_vma=False,
    )
```

```python
import functools

import jax
import jax.numpy as jnp
from jax import lax
from jax.experimental import pallas as pl
from jax.experimental.pallas import tpu as pltpu
from jax.sharding import PartitionSpec as P

HD = 64
BLK = 128
NNZ = 2
LANES = 128
QUADS = 4
HEAD_BIT = 2
NT = (((1,), (1,)), ((), ()))
ORDER = (2, 3, 1)
VMEM_LIMIT = 24 * 1024 * 1024
PACK_LIMIT = 60 * 1024 * 1024


def vmem():
    return pl.BlockSpec(memory_space=pltpu.VMEM)


def smem():
    return pl.BlockSpec(memory_space=pltpu.SMEM)


def hbm():
    return pl.BlockSpec(memory_space=pltpu.HBM)


def flips_of(seq_size):
    flips = [0]
    bit = 1
    while bit < seq_size:
        if bit not in (HEAD_BIT, 2 * HEAD_BIT):
            flips = flips + [f ^ bit for f in flips]
        bit *= 2
    return flips


def exchange(x, axis, size, flip):
    return lax.ppermute(x, axis, [(i, i ^ flip) for i in range(size)])


def after(x, *earlier):
    return lax.optimization_barrier((x, *earlier))[0]


def butterfly(x, axis, size, bits):
    held = [x]
    for bit in bits:
        held = held + [exchange(part, axis, size, bit) for part in held]
    return held


def mask_rows(seq_size):
    return 16 * ((seq_size + 15) // 16)


def pack_kernel(seq_size, q_ref, k_ref, v_ref, mask_ref, *outs):
    me = lax.axis_index("seq")
    group = lax.rem(me // HEAD_BIT, QUADS)
    rows = mask_rows(seq_size)
    row_id = lax.broadcasted_iota(jnp.int32, (rows, LANES), 0)
    for s in range(QUADS):
        cols = pl.ds(pl.multiple_of(lax.bitwise_xor(group, s) * LANES, LANES), LANES)
        for i, ref in enumerate((q_ref, k_ref, v_ref)):
            outs[s][i * BLK : (i + 1) * BLK, :] = ref[0, :, cols]
        there = lax.bitwise_xor(me, s * HEAD_BIT)
        allowed = jnp.zeros((rows, LANES), jnp.float32)
        for t, flip in enumerate(flips_of(seq_size)):
            for u in range(QUADS):
                block = lax.bitwise_xor(there, flip ^ (u * HEAD_BIT))
                bit = mask_ref[0, 0, block].astype(jnp.float32)
                allowed = jnp.where(row_id == t * QUADS + u, bit, allowed)
        outs[s][3 * BLK :, :] = allowed.astype(jnp.bfloat16)


def pack(query, key, value, attn_mask, seq_size):
    rows = 3 * BLK + mask_rows(seq_size)
    return pl.pallas_call(
        functools.partial(pack_kernel, seq_size),
        out_shape=[jax.ShapeDtypeStruct((rows, LANES), jnp.bfloat16)] * QUADS,
        in_specs=[vmem(), vmem(), vmem(), smem()],
        out_specs=[vmem()] * QUADS,
        compiler_params=pltpu.CompilerParams(vmem_limit_bytes=PACK_LIMIT),
        name="pack",
    )(query, key, value, attn_mask)


def attend_kernel(first, last, parts, *refs):
    q_refs, refs = refs[:QUADS], refs[QUADS:]
    if first:
        rows_ref, cols_ref, gain_ref = refs[:3]
        refs = refs[3:]
        refs[3][0:NNZ, :] = rows_ref[...]
        refs[3][NNZ:, :] = cols_ref[...]
        refs[4][...] = gain_ref[...]
    else:
        kv_refs, refs = refs[: QUADS * parts], refs[QUADS * parts :]
        state_refs, refs = refs[:3], refs[3:]
    scale = HD**-0.5 * 1.4426950408889634
    first_head = lax.broadcasted_iota(jnp.int32, (BLK, LANES), 1) < HD
    for s in range(QUADS):
        q = q_refs[s][0:BLK, :]
        zero = jnp.zeros_like(q)
        both = jnp.concatenate(
            [jnp.where(first_head, q, zero), jnp.where(first_head, zero, q)], axis=0
        )
        allowed = q_refs[s][3 * BLK :, :].astype(jnp.float32)
        if first:
            pairs = [(q_refs[u][BLK : 2 * BLK, :], q_refs[u][2 * BLK : 3 * BLK, :]) for u in range(QUADS)]
            base = 0
        else:
            pairs = [(ref[0:BLK, :], ref[BLK : 2 * BLK, :]) for ref in kv_refs]
            base = QUADS
        scores = []
        for row, (key, _) in enumerate(pairs):
            dots = lax.dot_general(both, key, NT, preferred_element_type=jnp.float32)
            scores.append(jnp.where(allowed[base + row : base + row + 1, :] > 0, dots, -1e30))
        top = functools.reduce(jnp.maximum, scores)
        if not first:
            top = jnp.maximum(top, state_refs[0][s])
        top = jnp.max(top, axis=1, keepdims=True)
        if first:
            total = jnp.zeros((2 * BLK, LANES), jnp.float32)
            mixed = jnp.zeros((2 * BLK, LANES), jnp.float32)
        else:
            shrink = jnp.exp2((state_refs[0][s] - top) * scale)
            total = state_refs[1][s] * shrink
            mixed = state_refs[2][s] * shrink
        for score, (_, value) in zip(scores, pairs):
            weight = jnp.exp2((score - top) * scale)
            total = total + weight
            mixed = mixed + jnp.dot(
                weight.astype(jnp.bfloat16), value, preferred_element_type=jnp.float32
            )
        if last:
            mixed = mixed / jnp.sum(total, axis=1, keepdims=True)
            refs[s][...] = jnp.where(first_head, mixed[:BLK], mixed[BLK:]).astype(jnp.bfloat16)
        else:
            refs[0][s] = jnp.broadcast_to(top, (2 * BLK, LANES))
            refs[1][s] = total
            refs[2][s] = mixed


def attend_own(packed, w1_rows, w2_cols, gain):
    return pl.pallas_call(
        functools.partial(attend_kernel, True, False, 1),
        out_shape=[jax.ShapeDtypeStruct((QUADS, 2 * BLK, LANES), jnp.float32)] * 3
        + [
            jax.ShapeDtypeStruct((2 * NNZ, w1_rows.shape[0]), jnp.int32),
            jax.ShapeDtypeStruct((1, gain.shape[0]), jnp.float32),
        ],
        in_specs=[vmem()] * (QUADS + 3),
        out_specs=[vmem()] * 5,
        compiler_params=pltpu.CompilerParams(vmem_limit_bytes=VMEM_LIMIT),
        cost_estimate=pl.CostEstimate(flops=2150000000, bytes_accessed=0, transcendentals=0),
        name="attend_own",
    )(*packed, w1_rows.T, w2_cols.T, gain[None])


def attend_rest(packed, rest, state):
    return pl.pallas_call(
        functools.partial(attend_kernel, False, True, len(rest) // QUADS),
        out_shape=[jax.ShapeDtypeStruct((BLK, LANES), jnp.bfloat16)] * QUADS,
        in_specs=[vmem()] * (QUADS + len(rest) + 3),
        out_specs=[vmem()] * QUADS,
        compiler_params=pltpu.CompilerParams(vmem_limit_bytes=VMEM_LIMIT),
        cost_estimate=pl.CostEstimate(flops=2150000000, bytes_accessed=0, transcendentals=0),
        name="attend_rest",
    )(*packed, *rest, *state)


def block_of(index):
    return pl.ds(pl.multiple_of(index * BLK, BLK), BLK)


def places(table_ref, owner, blocks, i):
    block = owner * blocks + i
    return (
        [table_ref[n, block] for n in range(NNZ)],
        [table_ref[NNZ + n, block] for n in range(NNZ)],
    )


def split_blocks(ref, blocks_ref):
    for d in range(blocks_ref.shape[0]):
        blocks_ref[d] = ref[0, :, d * BLK : (d + 1) * BLK]


def tall(ref, i):
    return ref[i].reshape(NNZ * BLK, BLK)


def wide(ref, i):
    return jnp.concatenate([ref[i, n] for n in range(NNZ)], axis=1)


def slope_terms(pre):
    cdf = 0.5 * (1.0 + lax.erf(pre * 0.7071067811865476))
    return pre * cdf, cdf + pre * jnp.exp(-0.5 * pre * pre) * 0.3989422804014327


def dact_of(grads_ref, second_ref, i, cols):
    grads = jnp.concatenate([grads_ref[c] for c in cols], axis=1)
    return lax.dot_general(grads, wide(second_ref, i), NT, preferred_element_type=jnp.float32)


def hidden_blocks(table_ref, owners, first_refs, second_refs, dact, normed_ref, act_ref, dpre_ref, mlp_ref, back_ref):
    blocks = first_refs[0].shape[0]
    steps = [(s, i) for s in range(len(owners)) for i in range(blocks)]
    for k, (s, i) in enumerate(steps):
        rows, cols = places(table_ref, owners[s], blocks, i)
        picked = jnp.concatenate([normed_ref[r] for r in rows], axis=1)
        pre = jnp.dot(picked, tall(first_refs[s], i), preferred_element_type=jnp.float32)
        act, slope = slope_terms(pre)
        act_ref[k] = act.astype(jnp.bfloat16)
        dpre_ref[k] = (dact(k, s, i, cols) * slope).astype(jnp.bfloat16)
    for k, (s, i) in enumerate(steps):
        rows, cols = places(table_ref, owners[s], blocks, i)
        forward = jnp.dot(act_ref[k], wide(second_refs[s], i), preferred_element_type=jnp.float32)
        backward = lax.dot_general(
            dpre_ref[k], tall(first_refs[s], i), NT, preferred_element_type=jnp.float32
        )
        for n in range(NNZ):
            mlp_ref[cols[n]] += forward[:, n * BLK : (n + 1) * BLK]
        for n in range(NNZ):
            back_ref[rows[n]] += backward[:, n * BLK : (n + 1) * BLK]


def near_kernel(near, table_in_ref, *refs):
    refs, (table_ref, table_sem) = refs[:-2], refs[-2:]
    table_copy = pltpu.make_async_copy(table_in_ref, table_ref, table_sem)
    table_copy.start()
    attn_refs, refs = refs[:QUADS], refs[QUADS:]
    proj_ref, tokens_ref, gain_ref, grad_ref = refs[:4]
    first_refs, second_refs = refs[4 : 4 + near], refs[4 + near : 4 + 3 * near]
    refs = refs[4 + 3 * near :]
    mlp_ref, back_ref, unit_ref, rstd_ref, normed_ref, far_dact_ref, act_ref, dpre_ref, grads_ref = refs
    split_blocks(grad_ref, grads_ref)
    group = lax.rem(lax.axis_index("seq") // HEAD_BIT, QUADS)
    hidden = tokens_ref[0].astype(jnp.float32)
    for s in range(QUADS):
        hidden = hidden + jnp.dot(
            attn_refs[s][...],
            proj_ref[block_of(lax.bitwise_xor(group, s)), :],
            preferred_element_type=jnp.float32,
        )
    mean = jnp.mean(hidden, axis=1, keepdims=True)
    centred = hidden - mean
    rstd = lax.rsqrt(jnp.mean(centred * centred, axis=1, keepdims=True) + 1e-06)
    unit = centred * rstd
    unit_ref[...] = unit
    rstd_ref[...] = jnp.broadcast_to(rstd, rstd_ref.shape)
    normed = (unit * gain_ref[...]).astype(jnp.bfloat16)
    for d in range(mlp_ref.shape[0]):
        normed_ref[d] = normed[:, d * BLK : (d + 1) * BLK]
        mlp_ref[d] = hidden[:, d * BLK : (d + 1) * BLK]
    back_ref[...] = jnp.zeros_like(back_ref)
    table_copy.wait()
    me = lax.axis_index("grp")
    owners = [lax.bitwise_xor(me, s) for s in range(2 * near)]
    blocks = first_refs[0].shape[0]
    hidden_blocks(
        table_ref,
        owners[:near],
        first_refs,
        second_refs[:near],
        lambda k, s, i, cols: dact_of(grads_ref, second_refs[s], i, cols),
        normed_ref,
        act_ref,
        dpre_ref,
        mlp_ref,
        back_ref,
    )
    for s in range(near):
        for i in range(blocks):
            _, cols = places(table_ref, owners[near + s], blocks, i)
            far_dact_ref[s * blocks + i] = dact_of(grads_ref, second_refs[near + s], i, cols)


def mlp_near(table, attn, out_proj, tokens, gain, grad_out, firsts, seconds):
    near = len(firsts)
    rows, width = tokens.shape[1:]
    kept = table.shape[1] // 2
    args = (*attn, out_proj, tokens, gain, grad_out, *firsts, *seconds)
    return pl.pallas_call(
        functools.partial(near_kernel, near),
        out_shape=[
            jax.ShapeDtypeStruct((width // BLK, rows, BLK), jnp.float32),
            jax.ShapeDtypeStruct((width // BLK, rows, BLK), jnp.float32),
            jax.ShapeDtypeStruct((rows, width), jnp.float32),
            jax.ShapeDtypeStruct((rows, LANES), jnp.float32),
            jax.ShapeDtypeStruct((width // BLK, rows, BLK), jnp.bfloat16),
            jax.ShapeDtypeStruct((kept, rows, BLK), jnp.float32),
        ],
        in_specs=[vmem()] * (1 + len(args)),
        out_specs=[vmem()] * 6,
        scratch_shapes=[pltpu.VMEM((kept, rows, BLK), jnp.bfloat16)] * 2
        + [pltpu.VMEM((width // BLK, rows, BLK), jnp.bfloat16)]
        + [pltpu.SMEM(table.shape, jnp.int32), pltpu.SemaphoreType.DMA],
        compiler_params=pltpu.CompilerParams(vmem_limit_bytes=VMEM_LIMIT),
        name="mlp_near",
    )(table, *args)


def far_kernel(near, table_in_ref, gain_ref, grad_ref, *refs):
    refs, (table_ref, table_sem) = refs[:-2], refs[-2:]
    table_copy = pltpu.make_async_copy(table_in_ref, table_ref, table_sem)
    table_copy.start()
    mlp_in_ref, back_in_ref, unit_ref, rstd_ref, normed_ref, dact_ref = refs[:6]
    first_refs, second_refs = refs[6 : 6 + near], refs[6 + near : 6 + 2 * near]
    out_ref, grad_out_ref, mlp_ref, back_ref, act_ref, dpre_ref = refs[6 + 2 * near :]
    mlp_ref[...] = mlp_in_ref[...]
    back_ref[...] = back_in_ref[...]
    table_copy.wait()
    me = lax.axis_index("grp")
    hidden_blocks(
        table_ref,
        [lax.bitwise_xor(me, near + s) for s in range(near)],
        first_refs,
        second_refs,
        lambda k, s, i, cols: dact_ref[k],
        normed_ref,
        act_ref,
        dpre_ref,
        mlp_ref,
        back_ref,
    )
    width_blocks = range(mlp_ref.shape[0])
    for d in width_blocks:
        out_ref[0, :, d * BLK : (d + 1) * BLK] = mlp_ref[d].astype(jnp.bfloat16)
    dxhat = jnp.concatenate([back_ref[d] for d in width_blocks], axis=1) * gain_ref[...]
    unit = unit_ref[...]
    dhidden = (
        dxhat
        - jnp.mean(dxhat, axis=1, keepdims=True)
        - unit * jnp.mean(dxhat * unit, axis=1, keepdims=True)
    )
    rstd = rstd_ref[:, 0:1]
    grad_out_ref[0] = (grad_ref[0].astype(jnp.float32) + rstd * dhidden).astype(jnp.bfloat16)


def mlp_far(table, gain, grad_out, state, firsts, seconds):
    near = len(firsts)
    shape = grad_out.shape
    kept = (table.shape[1] // 2, shape[1], BLK)
    args = (gain, grad_out, *state, *firsts, *seconds)
    return pl.pallas_call(
        functools.partial(far_kernel, near),
        out_shape=[jax.ShapeDtypeStruct(shape, jnp.bfloat16)] * 2,
        in_specs=[vmem()] * (1 + len(args)),
        out_specs=[vmem()] * 2,
        scratch_shapes=[pltpu.VMEM(state[0].shape, jnp.float32)] * 2
        + [pltpu.VMEM(kept, jnp.bfloat16)] * 2
        + [pltpu.SMEM(table.shape, jnp.int32), pltpu.SemaphoreType.DMA],
        compiler_params=pltpu.CompilerParams(vmem_limit_bytes=VMEM_LIMIT),
        name="mlp_far",
    )(table, *args)


def body(
    seq_size,
    grp_size,
    tokens,
    queries,
    keys,
    values,
    attn_mask,
    out_proj,
    norm_gain_vector,
    w1_packed,
    w1_rows,
    w2_packed,
    w2_cols,
    grad_out,
):
    flips = [f for f in flips_of(seq_size) if f and f & (f - 1) == 0]
    across = grp_size // 2
    near_bits = []
    bit = across // 2
    while bit:
        near_bits.append(bit)
        bit //= 2

    def over_seq(x, flip):
        return exchange(x, "seq", seq_size, flip)

    def over_grp(x, flip):
        return exchange(x, "grp", grp_size, flip)

    masks = [0]
    for bit in near_bits:
        masks = masks + [m ^ bit for m in masks]
    order = sorted(range(len(masks)), key=lambda i: masks[i])

    def over_near(x):
        held = butterfly(x, "grp", grp_size, near_bits)
        return [held[i] for i in order]

    far_second = over_grp(w2_packed, across)
    far_first = over_grp(w1_packed, across)
    packed = pack(queries, keys, values, attn_mask, seq_size)
    packed = {0: packed[0], **{s: over_seq(packed[s], s * HEAD_BIT) for s in ORDER}}
    packed = [packed[s] for s in range(QUADS)]
    held = [butterfly(p[BLK : 3 * BLK], "seq", seq_size, flips) for p in packed]
    near_seconds = over_near(after(w2_packed, *packed[1:]))
    near_firsts = over_near(after(w1_packed, *packed[1:]))
    *state, table, gain = attend_own(packed, w1_rows, w2_cols, norm_gain_vector)
    rest = [held[u][t] for t in range(1, len(held[0])) for u in range(QUADS)]
    far_seconds = over_near(after(far_second, state[0]))
    attn = attend_rest(packed, rest, state)
    attn = {0: attn[0], **{s: over_seq(attn[s], s * HEAD_BIT) for s in ORDER}}
    attn = [attn[s] for s in range(QUADS)]
    far_firsts = over_near(after(far_first, *attn[1:]))
    state = mlp_near(
        table, attn, out_proj, tokens, gain, grad_out, near_firsts, near_seconds + far_seconds
    )
    output, grad_tokens = mlp_far(table, gain, grad_out, state, far_firsts, far_seconds)
    return (output, grad_tokens)


def solution(mesh):
    return jax.shard_map(
        functools.partial(body, mesh.shape["seq"], mesh.shape["grp"]),
        mesh=mesh,
        in_specs=(
            P("grp", "seq", None),
            P("grp", "seq", None),
            P("grp", "seq", None),
            P("grp", "seq", None),
            P("grp", "seq", None),
            P(),
            P(),
            P("grp", None, None, None),
            P(),
            P("grp", None, None, None),
            P(),
            P("grp", "seq", None),
        ),
        out_specs=(P("grp", "seq", None), P("grp", "seq", None)),
        check_vma=False,
    )
```

```python
import functools

import jax
import jax.numpy as jnp
from jax import lax
from jax.experimental import pallas as pl
from jax.experimental.pallas import tpu as pltpu
from jax.sharding import PartitionSpec as P

HD = 64
BLK = 128
NNZ = 2
LANES = 128
QUADS = 4
HEAD_BIT = 2
NT = (((1,), (1,)), ((), ()))
ORDER = (2, 3, 1)
VMEM_LIMIT = 24 * 1024 * 1024
PACK_LIMIT = int(53.5 * 1024 * 1024)


def vmem():
    return pl.BlockSpec(memory_space=pltpu.VMEM)


def smem():
    return pl.BlockSpec(memory_space=pltpu.SMEM)


def hbm():
    return pl.BlockSpec(memory_space=pltpu.HBM)


def flips_of(seq_size):
    flips = [0]
    bit = 1
    while bit < seq_size:
        if bit not in (HEAD_BIT, 2 * HEAD_BIT):
            flips = flips + [f ^ bit for f in flips]
        bit *= 2
    return flips


def exchange(x, axis, size, flip):
    return lax.ppermute(x, axis, [(i, i ^ flip) for i in range(size)])


def after(x, *earlier):
    return lax.optimization_barrier((x, *earlier))[0]


def butterfly(x, axis, size, bits):
    held = [x]
    for bit in bits:
        held = held + [exchange(part, axis, size, bit) for part in held]
    return held


def mask_rows(seq_size):
    return 16 * ((seq_size + 15) // 16)


def pack_kernel(seq_size, q_ref, k_ref, v_ref, mask_ref, *outs):
    me = lax.axis_index("seq")
    group = lax.rem(me // HEAD_BIT, QUADS)
    rows = mask_rows(seq_size)
    row_id = lax.broadcasted_iota(jnp.int32, (rows, LANES), 0)
    for s in range(QUADS):
        cols = pl.ds(pl.multiple_of(lax.bitwise_xor(group, s) * LANES, LANES), LANES)
        for i, ref in enumerate((q_ref, k_ref, v_ref)):
            outs[s][i * BLK : (i + 1) * BLK, :] = ref[0, :, cols]
        there = lax.bitwise_xor(me, s * HEAD_BIT)
        allowed = jnp.zeros((rows, LANES), jnp.float32)
        for t, flip in enumerate(flips_of(seq_size)):
            for u in range(QUADS):
                block = lax.bitwise_xor(there, flip ^ (u * HEAD_BIT))
                bit = mask_ref[0, 0, block].astype(jnp.float32)
                allowed = jnp.where(row_id == t * QUADS + u, bit, allowed)
        outs[s][3 * BLK :, :] = allowed.astype(jnp.bfloat16)


def pack(query, key, value, attn_mask, seq_size):
    rows = 3 * BLK + mask_rows(seq_size)
    return pl.pallas_call(
        functools.partial(pack_kernel, seq_size),
        out_shape=[jax.ShapeDtypeStruct((rows, LANES), jnp.bfloat16)] * QUADS,
        in_specs=[vmem(), vmem(), vmem(), smem()],
        out_specs=[vmem()] * QUADS,
        compiler_params=pltpu.CompilerParams(vmem_limit_bytes=PACK_LIMIT),
        name="pack",
    )(query, key, value, attn_mask)


def attend_kernel(first, last, parts, *refs):
    q_refs, refs = refs[:QUADS], refs[QUADS:]
    if first:
        rows_ref, cols_ref, gain_ref = refs[:3]
        refs = refs[3:]
        refs[3][0:NNZ, :] = rows_ref[...]
        refs[3][NNZ:, :] = cols_ref[...]
        refs[4][...] = gain_ref[...]
    else:
        kv_refs, refs = refs[: QUADS * parts], refs[QUADS * parts :]
        state_refs, refs = refs[:3], refs[3:]
    scale = HD**-0.5 * 1.4426950408889634
    first_head = lax.broadcasted_iota(jnp.int32, (BLK, LANES), 1) < HD
    for s in range(QUADS):
        q = q_refs[s][0:BLK, :]
        zero = jnp.zeros_like(q)
        both = jnp.concatenate(
            [jnp.where(first_head, q, zero), jnp.where(first_head, zero, q)], axis=0
        )
        allowed = q_refs[s][3 * BLK :, :].astype(jnp.float32)
        if first:
            pairs = [(q_refs[u][BLK : 2 * BLK, :], q_refs[u][2 * BLK : 3 * BLK, :]) for u in range(QUADS)]
            base = 0
        else:
            pairs = [(ref[0:BLK, :], ref[BLK : 2 * BLK, :]) for ref in kv_refs]
            base = QUADS
        scores = []
        for row, (key, _) in enumerate(pairs):
            dots = lax.dot_general(both, key, NT, preferred_element_type=jnp.float32)
            scores.append(jnp.where(allowed[base + row : base + row + 1, :] > 0, dots, -1e30))
        top = functools.reduce(jnp.maximum, scores)
        if not first:
            top = jnp.maximum(top, state_refs[0][s])
        top = jnp.max(top, axis=1, keepdims=True)
        if first:
            total = jnp.zeros((2 * BLK, LANES), jnp.float32)
            mixed = jnp.zeros((2 * BLK, LANES), jnp.float32)
        else:
            shrink = jnp.exp2((state_refs[0][s] - top) * scale)
            total = state_refs[1][s] * shrink
            mixed = state_refs[2][s] * shrink
        for score, (_, value) in zip(scores, pairs):
            weight = jnp.exp2((score - top) * scale)
            total = total + weight
            mixed = mixed + jnp.dot(
                weight.astype(jnp.bfloat16), value, preferred_element_type=jnp.float32
            )
        if last:
            mixed = mixed / jnp.sum(total, axis=1, keepdims=True)
            refs[s][...] = jnp.where(first_head, mixed[:BLK], mixed[BLK:]).astype(jnp.bfloat16)
        else:
            refs[0][s] = jnp.broadcast_to(top, (2 * BLK, LANES))
            refs[1][s] = total
            refs[2][s] = mixed


def attend_own(packed, w1_rows, w2_cols, gain):
    return pl.pallas_call(
        functools.partial(attend_kernel, True, False, 1),
        out_shape=[jax.ShapeDtypeStruct((QUADS, 2 * BLK, LANES), jnp.float32)] * 3
        + [
            jax.ShapeDtypeStruct((2 * NNZ, w1_rows.shape[0]), jnp.int32),
            jax.ShapeDtypeStruct((1, gain.shape[0]), jnp.float32),
        ],
        in_specs=[vmem()] * (QUADS + 3),
        out_specs=[vmem()] * 5,
        compiler_params=pltpu.CompilerParams(vmem_limit_bytes=VMEM_LIMIT),
        cost_estimate=pl.CostEstimate(flops=2150000000, bytes_accessed=0, transcendentals=0),
        name="attend_own",
    )(*packed, w1_rows.T, w2_cols.T, gain[None])


def attend_rest(packed, rest, state):
    return pl.pallas_call(
        functools.partial(attend_kernel, False, True, len(rest) // QUADS),
        out_shape=[jax.ShapeDtypeStruct((BLK, LANES), jnp.bfloat16)] * QUADS,
        in_specs=[vmem()] * (QUADS + len(rest) + 3),
        out_specs=[vmem()] * QUADS,
        compiler_params=pltpu.CompilerParams(vmem_limit_bytes=VMEM_LIMIT),
        cost_estimate=pl.CostEstimate(flops=2150000000, bytes_accessed=0, transcendentals=0),
        name="attend_rest",
    )(*packed, *rest, *state)


def block_of(index):
    return pl.ds(pl.multiple_of(index * BLK, BLK), BLK)


def places(table_ref, owner, blocks, i):
    block = owner * blocks + i
    return (
        [table_ref[n, block] for n in range(NNZ)],
        [table_ref[NNZ + n, block] for n in range(NNZ)],
    )


def split_blocks(ref, blocks_ref):
    for d in range(blocks_ref.shape[0]):
        blocks_ref[d] = ref[0, :, d * BLK : (d + 1) * BLK]


def tall(ref, i):
    return ref[i].reshape(NNZ * BLK, BLK)


def wide(ref, i):
    return jnp.concatenate([ref[i, n] for n in range(NNZ)], axis=1)


def slope_terms(pre):
    cdf = 0.5 * (1.0 + lax.erf(pre * 0.7071067811865476))
    return pre * cdf, cdf + pre * jnp.exp(-0.5 * pre * pre) * 0.3989422804014327


def dact_of(grads_ref, second_ref, i, cols):
    grads = jnp.concatenate([grads_ref[c] for c in cols], axis=1)
    return lax.dot_general(grads, wide(second_ref, i), NT, preferred_element_type=jnp.float32)


def hidden_blocks(table_ref, owners, first_refs, second_refs, dact, normed_ref, act_ref, dpre_ref, mlp_ref, back_ref):
    blocks = first_refs[0].shape[0]
    steps = [(s, i) for s in range(len(owners)) for i in range(blocks)]
    for k, (s, i) in enumerate(steps):
        rows, cols = places(table_ref, owners[s], blocks, i)
        picked = jnp.concatenate([normed_ref[r] for r in rows], axis=1)
        pre = jnp.dot(picked, tall(first_refs[s], i), preferred_element_type=jnp.float32)
        act, slope = slope_terms(pre)
        act_ref[k] = act.astype(jnp.bfloat16)
        dpre_ref[k] = (dact(k, s, i, cols) * slope).astype(jnp.bfloat16)
    for k, (s, i) in enumerate(steps):
        rows, cols = places(table_ref, owners[s], blocks, i)
        forward = jnp.dot(act_ref[k], wide(second_refs[s], i), preferred_element_type=jnp.float32)
        backward = lax.dot_general(
            dpre_ref[k], tall(first_refs[s], i), NT, preferred_element_type=jnp.float32
        )
        for n in range(NNZ):
            mlp_ref[cols[n]] += forward[:, n * BLK : (n + 1) * BLK]
        for n in range(NNZ):
            back_ref[rows[n]] += backward[:, n * BLK : (n + 1) * BLK]


def near_kernel(near, table_in_ref, *refs):
    refs, (table_ref, table_sem) = refs[:-2], refs[-2:]
    table_copy = pltpu.make_async_copy(table_in_ref, table_ref, table_sem)
    table_copy.start()
    attn_refs, refs = refs[:QUADS], refs[QUADS:]
    proj_ref, tokens_ref, gain_ref, grad_ref = refs[:4]
    first_refs, second_refs = refs[4 : 4 + near], refs[4 + near : 4 + 3 * near]
    refs = refs[4 + 3 * near :]
    mlp_ref, back_ref, unit_ref, rstd_ref, normed_ref, far_dact_ref, act_ref, dpre_ref, grads_ref = refs
    split_blocks(grad_ref, grads_ref)
    group = lax.rem(lax.axis_index("seq") // HEAD_BIT, QUADS)
    hidden = tokens_ref[0].astype(jnp.float32)
    for s in range(QUADS):
        hidden = hidden + jnp.dot(
            attn_refs[s][...],
            proj_ref[block_of(lax.bitwise_xor(group, s)), :],
            preferred_element_type=jnp.float32,
        )
    mean = jnp.mean(hidden, axis=1, keepdims=True)
    centred = hidden - mean
    rstd = lax.rsqrt(jnp.mean(centred * centred, axis=1, keepdims=True) + 1e-06)
    unit = centred * rstd
    unit_ref[...] = unit
    rstd_ref[...] = jnp.broadcast_to(rstd, rstd_ref.shape)
    normed = (unit * gain_ref[...]).astype(jnp.bfloat16)
    for d in range(mlp_ref.shape[0]):
        normed_ref[d] = normed[:, d * BLK : (d + 1) * BLK]
        mlp_ref[d] = hidden[:, d * BLK : (d + 1) * BLK]
    back_ref[...] = jnp.zeros_like(back_ref)
    table_copy.wait()
    me = lax.axis_index("grp")
    owners = [lax.bitwise_xor(me, s) for s in range(2 * near)]
    blocks = first_refs[0].shape[0]
    hidden_blocks(
        table_ref,
        owners[:near],
        first_refs,
        second_refs[:near],
        lambda k, s, i, cols: dact_of(grads_ref, second_refs[s], i, cols),
        normed_ref,
        act_ref,
        dpre_ref,
        mlp_ref,
        back_ref,
    )
    for s in range(near):
        for i in range(blocks):
            _, cols = places(table_ref, owners[near + s], blocks, i)
            far_dact_ref[s * blocks + i] = dact_of(grads_ref, second_refs[near + s], i, cols)


def mlp_near(table, attn, out_proj, tokens, gain, grad_out, firsts, seconds):
    near = len(firsts)
    rows, width = tokens.shape[1:]
    kept = table.shape[1] // 2
    args = (*attn, out_proj, tokens, gain, grad_out, *firsts, *seconds)
    return pl.pallas_call(
        functools.partial(near_kernel, near),
        out_shape=[
            jax.ShapeDtypeStruct((width // BLK, rows, BLK), jnp.float32),
            jax.ShapeDtypeStruct((width // BLK, rows, BLK), jnp.float32),
            jax.ShapeDtypeStruct((rows, width), jnp.float32),
            jax.ShapeDtypeStruct((rows, LANES), jnp.float32),
            jax.ShapeDtypeStruct((width // BLK, rows, BLK), jnp.bfloat16),
            jax.ShapeDtypeStruct((kept, rows, BLK), jnp.float32),
        ],
        in_specs=[vmem()] * (1 + len(args)),
        out_specs=[vmem()] * 6,
        scratch_shapes=[pltpu.VMEM((kept, rows, BLK), jnp.bfloat16)] * 2
        + [pltpu.VMEM((width // BLK, rows, BLK), jnp.bfloat16)]
        + [pltpu.SMEM(table.shape, jnp.int32), pltpu.SemaphoreType.DMA],
        compiler_params=pltpu.CompilerParams(vmem_limit_bytes=VMEM_LIMIT),
        name="mlp_near",
    )(table, *args)


def far_kernel(near, table_in_ref, gain_ref, grad_ref, *refs):
    refs, (table_ref, table_sem) = refs[:-2], refs[-2:]
    table_copy = pltpu.make_async_copy(table_in_ref, table_ref, table_sem)
    table_copy.start()
    mlp_in_ref, back_in_ref, unit_ref, rstd_ref, normed_ref, dact_ref = refs[:6]
    first_refs, second_refs = refs[6 : 6 + near], refs[6 + near : 6 + 2 * near]
    out_ref, grad_out_ref, mlp_ref, back_ref, act_ref, dpre_ref = refs[6 + 2 * near :]
    mlp_ref[...] = mlp_in_ref[...]
    back_ref[...] = back_in_ref[...]
    table_copy.wait()
    me = lax.axis_index("grp")
    hidden_blocks(
        table_ref,
        [lax.bitwise_xor(me, near + s) for s in range(near)],
        first_refs,
        second_refs,
        lambda k, s, i, cols: dact_ref[k],
        normed_ref,
        act_ref,
        dpre_ref,
        mlp_ref,
        back_ref,
    )
    width_blocks = range(mlp_ref.shape[0])
    for d in width_blocks:
        out_ref[0, :, d * BLK : (d + 1) * BLK] = mlp_ref[d].astype(jnp.bfloat16)
    dxhat = jnp.concatenate([back_ref[d] for d in width_blocks], axis=1) * gain_ref[...]
    unit = unit_ref[...]
    dhidden = (
        dxhat
        - jnp.mean(dxhat, axis=1, keepdims=True)
        - unit * jnp.mean(dxhat * unit, axis=1, keepdims=True)
    )
    rstd = rstd_ref[:, 0:1]
    grad_out_ref[0] = (grad_ref[0].astype(jnp.float32) + rstd * dhidden).astype(jnp.bfloat16)


def mlp_far(table, gain, grad_out, state, firsts, seconds):
    near = len(firsts)
    shape = grad_out.shape
    kept = (table.shape[1] // 2, shape[1], BLK)
    args = (gain, grad_out, *state, *firsts, *seconds)
    return pl.pallas_call(
        functools.partial(far_kernel, near),
        out_shape=[jax.ShapeDtypeStruct(shape, jnp.bfloat16)] * 2,
        in_specs=[vmem()] * (1 + len(args)),
        out_specs=[vmem()] * 2,
        scratch_shapes=[pltpu.VMEM(state[0].shape, jnp.float32)] * 2
        + [pltpu.VMEM(kept, jnp.bfloat16)] * 2
        + [pltpu.SMEM(table.shape, jnp.int32), pltpu.SemaphoreType.DMA],
        compiler_params=pltpu.CompilerParams(vmem_limit_bytes=VMEM_LIMIT),
        name="mlp_far",
    )(table, *args)


def body(
    seq_size,
    grp_size,
    tokens,
    queries,
    keys,
    values,
    attn_mask,
    out_proj,
    norm_gain_vector,
    w1_packed,
    w1_rows,
    w2_packed,
    w2_cols,
    grad_out,
):
    flips = [f for f in flips_of(seq_size) if f and f & (f - 1) == 0]
    across = grp_size // 2
    near_bits = []
    bit = across // 2
    while bit:
        near_bits.append(bit)
        bit //= 2

    def over_seq(x, flip):
        return exchange(x, "seq", seq_size, flip)

    def over_grp(x, flip):
        return exchange(x, "grp", grp_size, flip)

    masks = [0]
    for bit in near_bits:
        masks = masks + [m ^ bit for m in masks]
    order = sorted(range(len(masks)), key=lambda i: masks[i])

    def over_near(x):
        held = butterfly(x, "grp", grp_size, near_bits)
        return [held[i] for i in order]

    far_second = over_grp(w2_packed, across)
    far_first = over_grp(w1_packed, across)
    packed = pack(queries, keys, values, attn_mask, seq_size)
    packed = {0: packed[0], **{s: over_seq(packed[s], s * HEAD_BIT) for s in ORDER}}
    packed = [packed[s] for s in range(QUADS)]
    held = [butterfly(p[BLK : 3 * BLK], "seq", seq_size, flips) for p in packed]
    near_seconds = over_near(after(w2_packed, *packed[1:]))
    near_firsts = over_near(after(w1_packed, *packed[1:]))
    *state, table, gain = attend_own(packed, w1_rows, w2_cols, norm_gain_vector)
    rest = [held[u][t] for t in range(1, len(held[0])) for u in range(QUADS)]
    far_seconds = over_near(after(far_second, state[0]))
    attn = attend_rest(packed, rest, state)
    attn = {0: attn[0], **{s: over_seq(attn[s], s * HEAD_BIT) for s in ORDER}}
    attn = [attn[s] for s in range(QUADS)]
    far_firsts = over_near(after(far_first, *attn[1:]))
    state = mlp_near(
        table, attn, out_proj, tokens, gain, grad_out, near_firsts, near_seconds + far_seconds
    )
    output, grad_tokens = mlp_far(table, gain, grad_out, state, far_firsts, far_seconds)
    return (output, grad_tokens)


def solution(mesh):
    return jax.shard_map(
        functools.partial(body, mesh.shape["seq"], mesh.shape["grp"]),
        mesh=mesh,
        in_specs=(
            P("grp", "seq", None),
            P("grp", "seq", None),
            P("grp", "seq", None),
            P("grp", "seq", None),
            P("grp", "seq", None),
            P(),
            P(),
            P("grp", None, None, None),
            P(),
            P("grp", None, None, None),
            P(),
            P("grp", "seq", None),
        ),
        out_specs=(P("grp", "seq", None), P("grp", "seq", None)),
        check_vma=False,
    )
```

```python
import functools

import jax
import jax.numpy as jnp
from jax import lax
from jax.experimental import pallas as pl
from jax.experimental.pallas import tpu as pltpu
from jax.sharding import PartitionSpec as P

HD = 64
BLK = 128
NNZ = 2
LANES = 128
QUADS = 4
HEAD_BIT = 2
NT = (((1,), (1,)), ((), ()))
ORDER = (2, 3, 1)
VMEM_LIMIT = 24 * 1024 * 1024
PACK_LIMIT = int(53.5 * 1024 * 1024)


def vmem():
    return pl.BlockSpec(memory_space=pltpu.VMEM)


def smem():
    return pl.BlockSpec(memory_space=pltpu.SMEM)


def hbm():
    return pl.BlockSpec(memory_space=pltpu.HBM)


def flips_of(seq_size):
    flips = [0]
    bit = 1
    while bit < seq_size:
        if bit not in (HEAD_BIT, 2 * HEAD_BIT):
            flips = flips + [f ^ bit for f in flips]
        bit *= 2
    return flips


def exchange(x, axis, size, flip):
    return lax.ppermute(x, axis, [(i, i ^ flip) for i in range(size)])


def after(x, *earlier):
    return lax.optimization_barrier((x, *earlier))[0]


def butterfly(x, axis, size, bits):
    held = [x]
    for bit in bits:
        held = held + [exchange(part, axis, size, bit) for part in held]
    return held


def mask_rows(seq_size):
    return 16 * ((seq_size + 15) // 16)


def pack_kernel(seq_size, q_ref, k_ref, v_ref, mask_ref, *outs):
    me = lax.axis_index("seq")
    group = lax.rem(me // HEAD_BIT, QUADS)
    rows = mask_rows(seq_size)
    row_id = lax.broadcasted_iota(jnp.int32, (rows, LANES), 0)
    for s in range(QUADS):
        cols = pl.ds(pl.multiple_of(lax.bitwise_xor(group, s) * LANES, LANES), LANES)
        for i, ref in enumerate((q_ref, k_ref, v_ref)):
            outs[s][i * BLK : (i + 1) * BLK, :] = ref[0, :, cols]
        there = lax.bitwise_xor(me, s * HEAD_BIT)
        allowed = jnp.zeros((rows, LANES), jnp.float32)
        for t, flip in enumerate(flips_of(seq_size)):
            for u in range(QUADS):
                block = lax.bitwise_xor(there, flip ^ (u * HEAD_BIT))
                bit = mask_ref[0, 0, block].astype(jnp.float32)
                allowed = jnp.where(row_id == t * QUADS + u, bit, allowed)
        outs[s][3 * BLK :, :] = allowed.astype(jnp.bfloat16)


def pack(query, key, value, attn_mask, seq_size):
    rows = 3 * BLK + mask_rows(seq_size)
    return pl.pallas_call(
        functools.partial(pack_kernel, seq_size),
        out_shape=[jax.ShapeDtypeStruct((rows, LANES), jnp.bfloat16)] * QUADS,
        in_specs=[vmem(), vmem(), vmem(), smem()],
        out_specs=[vmem()] * QUADS,
        compiler_params=pltpu.CompilerParams(vmem_limit_bytes=PACK_LIMIT),
        name="pack",
    )(query, key, value, attn_mask)


def attend_kernel(first, last, parts, *refs):
    q_refs, refs = refs[:QUADS], refs[QUADS:]
    if first:
        rows_ref, cols_ref, gain_ref = refs[:3]
        refs = refs[3:]
        refs[3][0:NNZ, :] = rows_ref[...]
        refs[3][NNZ:, :] = cols_ref[...]
        refs[4][...] = gain_ref[...]
    else:
        kv_refs, refs = refs[: QUADS * parts], refs[QUADS * parts :]
        state_refs, refs = refs[:3], refs[3:]
    scale = HD**-0.5 * 1.4426950408889634
    first_head = lax.broadcasted_iota(jnp.int32, (BLK, LANES), 1) < HD
    for s in range(QUADS):
        q = q_refs[s][0:BLK, :]
        zero = jnp.zeros_like(q)
        both = jnp.concatenate(
            [jnp.where(first_head, q, zero), jnp.where(first_head, zero, q)], axis=0
        )
        allowed = q_refs[s][3 * BLK :, :].astype(jnp.float32)
        if first:
            pairs = [(q_refs[u][BLK : 2 * BLK, :], q_refs[u][2 * BLK : 3 * BLK, :]) for u in range(QUADS)]
            base = 0
        else:
            pairs = [(ref[0:BLK, :], ref[BLK : 2 * BLK, :]) for ref in kv_refs]
            base = QUADS
        scores = []
        for row, (key, _) in enumerate(pairs):
            dots = lax.dot_general(both, key, NT, preferred_element_type=jnp.float32)
            scores.append(jnp.where(allowed[base + row : base + row + 1, :] > 0, dots, -1e30))
        top = functools.reduce(jnp.maximum, scores)
        if not first:
            top = jnp.maximum(top, state_refs[0][s])
        top = jnp.max(top, axis=1, keepdims=True)
        if first:
            total = jnp.zeros((2 * BLK, LANES), jnp.float32)
            mixed = jnp.zeros((2 * BLK, LANES), jnp.float32)
        else:
            shrink = jnp.exp2((state_refs[0][s] - top) * scale)
            total = state_refs[1][s] * shrink
            mixed = state_refs[2][s] * shrink
        for score, (_, value) in zip(scores, pairs):
            weight = jnp.exp2((score - top) * scale)
            total = total + weight
            mixed = mixed + jnp.dot(
                weight.astype(jnp.bfloat16), value, preferred_element_type=jnp.float32
            )
        if last:
            mixed = mixed / jnp.sum(total, axis=1, keepdims=True)
            refs[s][...] = jnp.where(first_head, mixed[:BLK], mixed[BLK:]).astype(jnp.bfloat16)
        else:
            refs[0][s] = jnp.broadcast_to(top, (2 * BLK, LANES))
            refs[1][s] = total
            refs[2][s] = mixed


def attend_own(packed, w1_rows, w2_cols, gain):
    return pl.pallas_call(
        functools.partial(attend_kernel, True, False, 1),
        out_shape=[jax.ShapeDtypeStruct((QUADS, 2 * BLK, LANES), jnp.float32)] * 3
        + [
            jax.ShapeDtypeStruct((2 * NNZ, w1_rows.shape[0]), jnp.int32),
            jax.ShapeDtypeStruct((1, gain.shape[0]), jnp.float32),
        ],
        in_specs=[vmem()] * (QUADS + 3),
        out_specs=[vmem()] * 5,
        compiler_params=pltpu.CompilerParams(vmem_limit_bytes=VMEM_LIMIT),
        cost_estimate=pl.CostEstimate(flops=2150000000, bytes_accessed=0, transcendentals=0),
        name="attend_own",
    )(*packed, w1_rows.T, w2_cols.T, gain[None])


def attend_rest(packed, rest, state):
    return pl.pallas_call(
        functools.partial(attend_kernel, False, True, len(rest) // QUADS),
        out_shape=[jax.ShapeDtypeStruct((BLK, LANES), jnp.bfloat16)] * QUADS,
        in_specs=[vmem()] * (QUADS + len(rest) + 3),
        out_specs=[vmem()] * QUADS,
        compiler_params=pltpu.CompilerParams(vmem_limit_bytes=VMEM_LIMIT),
        cost_estimate=pl.CostEstimate(flops=2150000000, bytes_accessed=0, transcendentals=0),
        name="attend_rest",
    )(*packed, *rest, *state)


def block_of(index):
    return pl.ds(pl.multiple_of(index * BLK, BLK), BLK)


def places(table_ref, owner, blocks, i):
    block = owner * blocks + i
    return (
        [table_ref[n, block] for n in range(NNZ)],
        [table_ref[NNZ + n, block] for n in range(NNZ)],
    )


def split_blocks(ref, blocks_ref):
    for d in range(blocks_ref.shape[0]):
        blocks_ref[d] = ref[0, :, d * BLK : (d + 1) * BLK]


def tall(ref, i):
    return ref[i].reshape(NNZ * BLK, BLK)


def wide(ref, i):
    return jnp.concatenate([ref[i, n] for n in range(NNZ)], axis=1)


def slope_terms(pre):
    cdf = 0.5 * (1.0 + lax.erf(pre * 0.7071067811865476))
    return pre * cdf, cdf + pre * jnp.exp(-0.5 * pre * pre) * 0.3989422804014327


def dact_of(grads_ref, second_ref, i, cols):
    grads = jnp.concatenate([grads_ref[c] for c in cols], axis=1)
    return lax.dot_general(grads, wide(second_ref, i), NT, preferred_element_type=jnp.float32)


def hidden_blocks(table_ref, owners, first_refs, second_refs, dact, pick, act_ref, dpre_ref, mlp_ref, back_ref, table_ready=None):
    blocks = first_refs[0].shape[0]
    steps = [(s, i) for s in range(len(owners)) for i in range(blocks)]
    for k, (s, i) in enumerate(steps):
        rows, cols = places(table_ref, owners[s], blocks, i) if table_ready is None else (None, None)
        picked = pick(k, rows)
        pre = jnp.dot(picked, tall(first_refs[s], i), preferred_element_type=jnp.float32)
        act, slope = slope_terms(pre)
        act_ref[k] = act.astype(jnp.bfloat16)
        dpre_ref[k] = (dact(k, s, i, cols) * slope).astype(jnp.bfloat16)
    if table_ready is not None:
        table_ready()
    for k, (s, i) in enumerate(steps):
        rows, cols = places(table_ref, owners[s], blocks, i)
        forward = jnp.dot(act_ref[k], wide(second_refs[s], i), preferred_element_type=jnp.float32)
        backward = lax.dot_general(
            dpre_ref[k], tall(first_refs[s], i), NT, preferred_element_type=jnp.float32
        )
        for n in range(NNZ):
            mlp_ref[cols[n]] += forward[:, n * BLK : (n + 1) * BLK]
        for n in range(NNZ):
            back_ref[rows[n]] += backward[:, n * BLK : (n + 1) * BLK]


def near_kernel(near, table_in_ref, *refs):
    refs, (table_ref, table_sem) = refs[:-2], refs[-2:]
    table_copy = pltpu.make_async_copy(table_in_ref, table_ref, table_sem)
    table_copy.start()
    attn_refs, refs = refs[:QUADS], refs[QUADS:]
    proj_ref, tokens_ref, gain_ref, grad_ref = refs[:4]
    first_refs, second_refs = refs[4 : 4 + near], refs[4 + near : 4 + 3 * near]
    refs = refs[4 + 3 * near :]
    mlp_ref, back_ref, unit_ref, rstd_ref, far_picked_ref, far_dact_ref, normed_ref, act_ref, dpre_ref, grads_ref = refs
    split_blocks(grad_ref, grads_ref)
    group = lax.rem(lax.axis_index("seq") // HEAD_BIT, QUADS)
    hidden = tokens_ref[0].astype(jnp.float32)
    for s in range(QUADS):
        hidden = hidden + jnp.dot(
            attn_refs[s][...],
            proj_ref[block_of(lax.bitwise_xor(group, s)), :],
            preferred_element_type=jnp.float32,
        )
    mean = jnp.mean(hidden, axis=1, keepdims=True)
    centred = hidden - mean
    rstd = lax.rsqrt(jnp.mean(centred * centred, axis=1, keepdims=True) + 1e-06)
    unit = centred * rstd
    unit_ref[...] = unit
    rstd_ref[...] = jnp.broadcast_to(rstd, rstd_ref.shape)
    normed = (unit * gain_ref[...]).astype(jnp.bfloat16)
    for d in range(mlp_ref.shape[0]):
        normed_ref[d] = normed[:, d * BLK : (d + 1) * BLK]
        mlp_ref[d] = hidden[:, d * BLK : (d + 1) * BLK]
    back_ref[...] = jnp.zeros_like(back_ref)
    table_copy.wait()
    me = lax.axis_index("grp")
    owners = [lax.bitwise_xor(me, s) for s in range(2 * near)]
    blocks = first_refs[0].shape[0]
    hidden_blocks(
        table_ref,
        owners[:near],
        first_refs,
        second_refs[:near],
        lambda k, s, i, cols: dact_of(grads_ref, second_refs[s], i, cols),
        lambda k, rows: jnp.concatenate([normed_ref[r] for r in rows], axis=1),
        act_ref,
        dpre_ref,
        mlp_ref,
        back_ref,
    )
    for s in range(near):
        for i in range(blocks):
            rows, cols = places(table_ref, owners[near + s], blocks, i)
            picked = jnp.concatenate([normed_ref[r] for r in rows], axis=1)
            far_picked_ref[s * blocks + i] = picked
            far_dact_ref[s * blocks + i] = dact_of(grads_ref, second_refs[near + s], i, cols)


def mlp_near(table, attn, out_proj, tokens, gain, grad_out, firsts, seconds):
    near = len(firsts)
    rows, width = tokens.shape[1:]
    kept = table.shape[1] // 2
    args = (*attn, out_proj, tokens, gain, grad_out, *firsts, *seconds)
    return pl.pallas_call(
        functools.partial(near_kernel, near),
        out_shape=[
            jax.ShapeDtypeStruct((width // BLK, rows, BLK), jnp.float32),
            jax.ShapeDtypeStruct((width // BLK, rows, BLK), jnp.float32),
            jax.ShapeDtypeStruct((rows, width), jnp.float32),
            jax.ShapeDtypeStruct((rows, LANES), jnp.float32),
            jax.ShapeDtypeStruct((kept, rows, NNZ * BLK), jnp.bfloat16),
            jax.ShapeDtypeStruct((kept, rows, BLK), jnp.float32),
        ],
        in_specs=[vmem()] * (1 + len(args)),
        out_specs=[vmem()] * 6,
        scratch_shapes=[pltpu.VMEM((width // BLK, rows, BLK), jnp.bfloat16)]
        + [pltpu.VMEM((kept, rows, BLK), jnp.bfloat16)] * 2
        + [pltpu.VMEM((width // BLK, rows, BLK), jnp.bfloat16)]
        + [pltpu.SMEM(table.shape, jnp.int32), pltpu.SemaphoreType.DMA],
        compiler_params=pltpu.CompilerParams(vmem_limit_bytes=VMEM_LIMIT),
        name="mlp_near",
    )(table, *args)


def far_kernel(near, table_in_ref, gain_ref, grad_ref, *refs):
    refs, (table_ref, table_sem) = refs[:-2], refs[-2:]
    table_copy = pltpu.make_async_copy(table_in_ref, table_ref, table_sem)
    table_copy.start()
    mlp_in_ref, back_in_ref, unit_ref, rstd_ref, picked_ref, dact_ref = refs[:6]
    first_refs, second_refs = refs[6 : 6 + near], refs[6 + near : 6 + 2 * near]
    out_ref, grad_out_ref, mlp_ref, back_ref, act_ref, dpre_ref = refs[6 + 2 * near :]
    mlp_ref[...] = mlp_in_ref[...]
    back_ref[...] = back_in_ref[...]
    me = lax.axis_index("grp")
    hidden_blocks(
        table_ref,
        [lax.bitwise_xor(me, near + s) for s in range(near)],
        first_refs,
        second_refs,
        lambda k, s, i, cols: dact_ref[k],
        lambda k, rows: picked_ref[k],
        act_ref,
        dpre_ref,
        mlp_ref,
        back_ref,
        table_copy.wait,
    )
    width_blocks = range(mlp_ref.shape[0])
    for d in width_blocks:
        out_ref[0, :, d * BLK : (d + 1) * BLK] = mlp_ref[d].astype(jnp.bfloat16)
    dxhat = jnp.concatenate([back_ref[d] for d in width_blocks], axis=1) * gain_ref[...]
    unit = unit_ref[...]
    dhidden = (
        dxhat
        - jnp.mean(dxhat, axis=1, keepdims=True)
        - unit * jnp.mean(dxhat * unit, axis=1, keepdims=True)
    )
    rstd = rstd_ref[:, 0:1]
    grad_out_ref[0] = (grad_ref[0].astype(jnp.float32) + rstd * dhidden).astype(jnp.bfloat16)


def mlp_far(table, gain, grad_out, state, firsts, seconds):
    near = len(firsts)
    shape = grad_out.shape
    kept = (table.shape[1] // 2, shape[1], BLK)
    args = (gain, grad_out, *state, *firsts, *seconds)
    return pl.pallas_call(
        functools.partial(far_kernel, near),
        out_shape=[jax.ShapeDtypeStruct(shape, jnp.bfloat16)] * 2,
        in_specs=[vmem()] * (1 + len(args)),
        out_specs=[vmem()] * 2,
        scratch_shapes=[pltpu.VMEM(state[0].shape, jnp.float32)] * 2
        + [pltpu.VMEM(kept, jnp.bfloat16)] * 2
        + [pltpu.SMEM(table.shape, jnp.int32), pltpu.SemaphoreType.DMA],
        compiler_params=pltpu.CompilerParams(vmem_limit_bytes=VMEM_LIMIT),
        name="mlp_far",
    )(table, *args)


def body(
    seq_size,
    grp_size,
    tokens,
    queries,
    keys,
    values,
    attn_mask,
    out_proj,
    norm_gain_vector,
    w1_packed,
    w1_rows,
    w2_packed,
    w2_cols,
    grad_out,
):
    flips = [f for f in flips_of(seq_size) if f and f & (f - 1) == 0]
    across = grp_size // 2
    near_bits = []
    bit = across // 2
    while bit:
        near_bits.append(bit)
        bit //= 2

    def over_seq(x, flip):
        return exchange(x, "seq", seq_size, flip)

    def over_grp(x, flip):
        return exchange(x, "grp", grp_size, flip)

    masks = [0]
    for bit in near_bits:
        masks = masks + [m ^ bit for m in masks]
    order = sorted(range(len(masks)), key=lambda i: masks[i])

    def over_near(x):
        held = butterfly(x, "grp", grp_size, near_bits)
        return [held[i] for i in order]

    far_second = over_grp(w2_packed, across)
    far_first = over_grp(w1_packed, across)
    packed = pack(queries, keys, values, attn_mask, seq_size)
    packed = {0: packed[0], **{s: over_seq(packed[s], s * HEAD_BIT) for s in ORDER}}
    packed = [packed[s] for s in range(QUADS)]
    held = [butterfly(p[BLK : 3 * BLK], "seq", seq_size, flips) for p in packed]
    near_seconds = over_near(after(w2_packed, *packed[1:]))
    near_firsts = over_near(after(w1_packed, *packed[1:]))
    *state, table, gain = attend_own(packed, w1_rows, w2_cols, norm_gain_vector)
    rest = [held[u][t] for t in range(1, len(held[0])) for u in range(QUADS)]
    far_seconds = over_near(after(far_second, state[0]))
    attn = attend_rest(packed, rest, state)
    attn = {0: attn[0], **{s: over_seq(attn[s], s * HEAD_BIT) for s in ORDER}}
    attn = [attn[s] for s in range(QUADS)]
    far_firsts = over_near(after(far_first, *attn[1:]))
    state = mlp_near(
        table, attn, out_proj, tokens, gain, grad_out, near_firsts, near_seconds + far_seconds
    )
    output, grad_tokens = mlp_far(table, gain, grad_out, state, far_firsts, far_seconds)
    return (output, grad_tokens)


def solution(mesh):
    return jax.shard_map(
        functools.partial(body, mesh.shape["seq"], mesh.shape["grp"]),
        mesh=mesh,
        in_specs=(
            P("grp", "seq", None),
            P("grp", "seq", None),
            P("grp", "seq", None),
            P("grp", "seq", None),
            P("grp", "seq", None),
            P(),
            P(),
            P("grp", None, None, None),
            P(),
            P("grp", None, None, None),
            P(),
            P("grp", "seq", None),
        ),
        out_specs=(P("grp", "seq", None), P("grp", "seq", None)),
        check_vma=False,
    )
```

```python
import functools

import jax
import jax.numpy as jnp
from jax import lax
from jax.experimental import pallas as pl
from jax.experimental.pallas import tpu as pltpu
from jax.sharding import PartitionSpec as P

HD = 64
BLK = 128
NNZ = 2
LANES = 128
QUADS = 4
HEAD_BIT = 2
NT = (((1,), (1,)), ((), ()))
ORDER = (2, 3, 1)
VMEM_LIMIT = 24 * 1024 * 1024
PACK_LIMIT = int(53.5 * 1024 * 1024)


def vmem():
    return pl.BlockSpec(memory_space=pltpu.VMEM)


def smem():
    return pl.BlockSpec(memory_space=pltpu.SMEM)


def hbm():
    return pl.BlockSpec(memory_space=pltpu.HBM)


def flips_of(seq_size):
    flips = [0]
    bit = 1
    while bit < seq_size:
        if bit not in (HEAD_BIT, 2 * HEAD_BIT):
            flips = flips + [f ^ bit for f in flips]
        bit *= 2
    return flips


def exchange(x, axis, size, flip):
    return lax.ppermute(x, axis, [(i, i ^ flip) for i in range(size)])


def after(x, *earlier):
    return lax.optimization_barrier((x, *earlier))[0]


def butterfly(x, axis, size, bits):
    held = [x]
    for bit in bits:
        held = held + [exchange(part, axis, size, bit) for part in held]
    return held


def mask_rows(seq_size):
    return 16 * ((seq_size + 15) // 16)


def pack_kernel(seq_size, q_ref, k_ref, v_ref, mask_ref, *outs):
    me = lax.axis_index("seq")
    group = lax.rem(me // HEAD_BIT, QUADS)
    rows = mask_rows(seq_size)
    row_id = lax.broadcasted_iota(jnp.int32, (rows, LANES), 0)
    for s in range(QUADS):
        cols = pl.ds(pl.multiple_of(lax.bitwise_xor(group, s) * LANES, LANES), LANES)
        for i, ref in enumerate((q_ref, k_ref, v_ref)):
            outs[s][i * BLK : (i + 1) * BLK, :] = ref[0, :, cols]
        there = lax.bitwise_xor(me, s * HEAD_BIT)
        allowed = jnp.zeros((rows, LANES), jnp.float32)
        for t, flip in enumerate(flips_of(seq_size)):
            for u in range(QUADS):
                block = lax.bitwise_xor(there, flip ^ (u * HEAD_BIT))
                bit = mask_ref[0, 0, block].astype(jnp.float32)
                allowed = jnp.where(row_id == t * QUADS + u, bit, allowed)
        outs[s][3 * BLK :, :] = allowed.astype(jnp.bfloat16)


def pack(query, key, value, attn_mask, seq_size):
    rows = 3 * BLK + mask_rows(seq_size)
    return pl.pallas_call(
        functools.partial(pack_kernel, seq_size),
        out_shape=[jax.ShapeDtypeStruct((rows, LANES), jnp.bfloat16)] * QUADS,
        in_specs=[vmem(), vmem(), vmem(), smem()],
        out_specs=[vmem()] * QUADS,
        compiler_params=pltpu.CompilerParams(vmem_limit_bytes=PACK_LIMIT),
        name="pack",
    )(query, key, value, attn_mask)


def attend_kernel(first, last, parts, *refs):
    q_refs, refs = refs[:QUADS], refs[QUADS:]
    if first:
        rows_ref, cols_ref, gain_ref = refs[:3]
        refs = refs[3:]
        refs[3][0:NNZ, :] = rows_ref[...]
        refs[3][NNZ:, :] = cols_ref[...]
        refs[4][...] = gain_ref[...]
    else:
        kv_refs, refs = refs[: QUADS * parts], refs[QUADS * parts :]
        state_refs, refs = refs[:3], refs[3:]
    scale = HD**-0.5 * 1.4426950408889634
    first_head = lax.broadcasted_iota(jnp.int32, (BLK, LANES), 1) < HD
    for s in range(QUADS):
        q = q_refs[s][0:BLK, :]
        zero = jnp.zeros_like(q)
        both = jnp.concatenate(
            [jnp.where(first_head, q, zero), jnp.where(first_head, zero, q)], axis=0
        )
        allowed = q_refs[s][3 * BLK :, :].astype(jnp.float32)
        if first:
            pairs = [(q_refs[u][BLK : 2 * BLK, :], q_refs[u][2 * BLK : 3 * BLK, :]) for u in range(QUADS)]
            base = 0
        else:
            pairs = [(ref[0:BLK, :], ref[BLK : 2 * BLK, :]) for ref in kv_refs]
            base = QUADS
        scores = []
        for row, (key, _) in enumerate(pairs):
            dots = lax.dot_general(both, key, NT, preferred_element_type=jnp.float32)
            scores.append(jnp.where(allowed[base + row : base + row + 1, :] > 0, dots, -1e30))
        top = functools.reduce(jnp.maximum, scores)
        if not first:
            top = jnp.maximum(top, state_refs[0][s])
        top = jnp.max(top, axis=1, keepdims=True)
        if first:
            total = jnp.zeros((2 * BLK, LANES), jnp.float32)
            mixed = jnp.zeros((2 * BLK, LANES), jnp.float32)
        else:
            shrink = jnp.exp2((state_refs[0][s] - top) * scale)
            total = state_refs[1][s] * shrink
            mixed = state_refs[2][s] * shrink
        for score, (_, value) in zip(scores, pairs):
            weight = jnp.exp2((score - top) * scale)
            total = total + weight
            mixed = mixed + jnp.dot(
                weight.astype(jnp.bfloat16), value, preferred_element_type=jnp.float32
            )
        if last:
            mixed = mixed / jnp.sum(total, axis=1, keepdims=True)
            refs[s][...] = jnp.where(first_head, mixed[:BLK], mixed[BLK:]).astype(jnp.bfloat16)
        else:
            refs[0][s] = jnp.broadcast_to(top, (2 * BLK, LANES))
            refs[1][s] = total
            refs[2][s] = mixed


def attend_own(packed, w1_rows, w2_cols, gain):
    return pl.pallas_call(
        functools.partial(attend_kernel, True, False, 1),
        out_shape=[jax.ShapeDtypeStruct((QUADS, 2 * BLK, LANES), jnp.float32)] * 3
        + [
            jax.ShapeDtypeStruct((2 * NNZ, w1_rows.shape[0]), jnp.int32),
            jax.ShapeDtypeStruct((1, gain.shape[0]), jnp.float32),
        ],
        in_specs=[vmem()] * (QUADS + 3),
        out_specs=[vmem()] * 5,
        compiler_params=pltpu.CompilerParams(vmem_limit_bytes=VMEM_LIMIT),
        cost_estimate=pl.CostEstimate(flops=2150000000, bytes_accessed=0, transcendentals=0),
        name="attend_own",
    )(*packed, w1_rows.T, w2_cols.T, gain[None])


def attend_rest(packed, rest, state):
    return pl.pallas_call(
        functools.partial(attend_kernel, False, True, len(rest) // QUADS),
        out_shape=[jax.ShapeDtypeStruct((BLK, LANES), jnp.bfloat16)] * QUADS,
        in_specs=[vmem()] * (QUADS + len(rest) + 3),
        out_specs=[vmem()] * QUADS,
        compiler_params=pltpu.CompilerParams(vmem_limit_bytes=VMEM_LIMIT),
        cost_estimate=pl.CostEstimate(flops=2150000000, bytes_accessed=0, transcendentals=0),
        name="attend_rest",
    )(*packed, *rest, *state)


def block_of(index):
    return pl.ds(pl.multiple_of(index * BLK, BLK), BLK)


def places(table_ref, owner, blocks, i):
    block = owner * blocks + i
    return (
        [table_ref[n, block] for n in range(NNZ)],
        [table_ref[NNZ + n, block] for n in range(NNZ)],
    )


def split_blocks(ref, blocks_ref):
    for d in range(blocks_ref.shape[0]):
        blocks_ref[d] = ref[0, :, d * BLK : (d + 1) * BLK]


def tall(ref, i):
    return ref[i].reshape(NNZ * BLK, BLK)


def wide(ref, i):
    return jnp.concatenate([ref[i, n] for n in range(NNZ)], axis=1)


def slope_terms(pre):
    cdf = 0.5 * (1.0 + lax.erf(pre * 0.7071067811865476))
    return pre * cdf, cdf + pre * jnp.exp(-0.5 * pre * pre) * 0.3989422804014327


def dact_of(grads_ref, second_ref, i, cols):
    grads = jnp.concatenate([grads_ref[c] for c in cols], axis=1)
    return lax.dot_general(grads, wide(second_ref, i), NT, preferred_element_type=jnp.float32)


def hidden_blocks(table_ref, owners, first_refs, second_refs, dact, pick, act_ref, dpre_ref, mlp_ref, back_ref, table_ready=None):
    blocks = first_refs[0].shape[0]
    steps = [(s, i) for s in range(len(owners)) for i in range(blocks)]
    for k, (s, i) in enumerate(steps):
        rows, cols = places(table_ref, owners[s], blocks, i) if table_ready is None else (None, None)
        picked = pick(k, rows)
        pre = jnp.dot(picked, tall(first_refs[s], i), preferred_element_type=jnp.float32)
        act, slope = slope_terms(pre)
        act_ref[k] = act.astype(jnp.bfloat16)
        dpre_ref[k] = (dact(k, s, i, cols) * slope).astype(jnp.bfloat16)
    if table_ready is not None:
        table_ready()
    for k, (s, i) in enumerate(steps):
        rows, cols = places(table_ref, owners[s], blocks, i)
        forward = jnp.dot(act_ref[k], wide(second_refs[s], i), preferred_element_type=jnp.float32)
        backward = lax.dot_general(
            dpre_ref[k], tall(first_refs[s], i), NT, preferred_element_type=jnp.float32
        )
        for n in range(NNZ):
            mlp_ref[cols[n]] += forward[:, n * BLK : (n + 1) * BLK]
        for n in range(NNZ):
            back_ref[rows[n]] += backward[:, n * BLK : (n + 1) * BLK]


def near_kernel(near, table_in_ref, *refs):
    refs, (table_ref, table_sem) = refs[:-2], refs[-2:]
    table_copy = pltpu.make_async_copy(table_in_ref, table_ref, table_sem)
    table_copy.start()
    attn_refs, refs = refs[:QUADS], refs[QUADS:]
    proj_ref, tokens_ref, gain_ref, grad_ref = refs[:4]
    first_refs, second_refs = refs[4 : 4 + near], refs[4 + near : 4 + 3 * near]
    refs = refs[4 + 3 * near :]
    mlp_ref, back_ref, unit_ref, rstd_ref, far_picked_ref, far_dact_ref, normed_ref, act_ref, dpre_ref, grads_ref = refs
    split_blocks(grad_ref, grads_ref)
    group = lax.rem(lax.axis_index("seq") // HEAD_BIT, QUADS)
    hidden = tokens_ref[0].astype(jnp.float32)
    places_of = [block_of(lax.bitwise_xor(group, s)) for s in range(QUADS)]
    hidden = hidden + jnp.dot(
        jnp.concatenate([ref[...] for ref in attn_refs], axis=1),
        jnp.concatenate([proj_ref[place, :] for place in places_of], axis=0),
        preferred_element_type=jnp.float32,
    )
    mean = jnp.mean(hidden, axis=1, keepdims=True)
    centred = hidden - mean
    rstd = lax.rsqrt(jnp.mean(centred * centred, axis=1, keepdims=True) + 1e-06)
    unit = centred * rstd
    unit_ref[...] = unit
    rstd_ref[...] = jnp.broadcast_to(rstd, rstd_ref.shape)
    normed = (unit * gain_ref[...]).astype(jnp.bfloat16)
    for d in range(mlp_ref.shape[0]):
        normed_ref[d] = normed[:, d * BLK : (d + 1) * BLK]
        mlp_ref[d] = hidden[:, d * BLK : (d + 1) * BLK]
    back_ref[...] = jnp.zeros_like(back_ref)
    table_copy.wait()
    me = lax.axis_index("grp")
    owners = [lax.bitwise_xor(me, s) for s in range(2 * near)]
    blocks = first_refs[0].shape[0]
    hidden_blocks(
        table_ref,
        owners[:near],
        first_refs,
        second_refs[:near],
        lambda k, s, i, cols: dact_of(grads_ref, second_refs[s], i, cols),
        lambda k, rows: jnp.concatenate([normed_ref[r] for r in rows], axis=1),
        act_ref,
        dpre_ref,
        mlp_ref,
        back_ref,
    )
    for s in range(near):
        for i in range(blocks):
            rows, cols = places(table_ref, owners[near + s], blocks, i)
            picked = jnp.concatenate([normed_ref[r] for r in rows], axis=1)
            far_picked_ref[s * blocks + i] = picked
            far_dact_ref[s * blocks + i] = dact_of(grads_ref, second_refs[near + s], i, cols)


def mlp_near(table, attn, out_proj, tokens, gain, grad_out, firsts, seconds):
    near = len(firsts)
    rows, width = tokens.shape[1:]
    kept = table.shape[1] // 2
    args = (*attn, out_proj, tokens, gain, grad_out, *firsts, *seconds)
    return pl.pallas_call(
        functools.partial(near_kernel, near),
        out_shape=[
            jax.ShapeDtypeStruct((width // BLK, rows, BLK), jnp.float32),
            jax.ShapeDtypeStruct((width // BLK, rows, BLK), jnp.float32),
            jax.ShapeDtypeStruct((rows, width), jnp.float32),
            jax.ShapeDtypeStruct((rows, LANES), jnp.float32),
            jax.ShapeDtypeStruct((kept, rows, NNZ * BLK), jnp.bfloat16),
            jax.ShapeDtypeStruct((kept, rows, BLK), jnp.float32),
        ],
        in_specs=[vmem()] * (1 + len(args)),
        out_specs=[vmem()] * 6,
        scratch_shapes=[pltpu.VMEM((width // BLK, rows, BLK), jnp.bfloat16)]
        + [pltpu.VMEM((kept, rows, BLK), jnp.bfloat16)] * 2
        + [pltpu.VMEM((width // BLK, rows, BLK), jnp.bfloat16)]
        + [pltpu.SMEM(table.shape, jnp.int32), pltpu.SemaphoreType.DMA],
        compiler_params=pltpu.CompilerParams(vmem_limit_bytes=VMEM_LIMIT),
        name="mlp_near",
    )(table, *args)


def far_kernel(near, table_in_ref, gain_ref, grad_ref, *refs):
    refs, (table_ref, table_sem) = refs[:-2], refs[-2:]
    table_copy = pltpu.make_async_copy(table_in_ref, table_ref, table_sem)
    table_copy.start()
    mlp_in_ref, back_in_ref, unit_ref, rstd_ref, picked_ref, dact_ref = refs[:6]
    first_refs, second_refs = refs[6 : 6 + near], refs[6 + near : 6 + 2 * near]
    out_ref, grad_out_ref, mlp_ref, back_ref, act_ref, dpre_ref = refs[6 + 2 * near :]
    mlp_ref[...] = mlp_in_ref[...]
    back_ref[...] = back_in_ref[...]
    me = lax.axis_index("grp")
    hidden_blocks(
        table_ref,
        [lax.bitwise_xor(me, near + s) for s in range(near)],
        first_refs,
        second_refs,
        lambda k, s, i, cols: dact_ref[k],
        lambda k, rows: picked_ref[k],
        act_ref,
        dpre_ref,
        mlp_ref,
        back_ref,
        table_copy.wait,
    )
    width_blocks = range(mlp_ref.shape[0])
    for d in width_blocks:
        out_ref[0, :, d * BLK : (d + 1) * BLK] = mlp_ref[d].astype(jnp.bfloat16)
    dxhat = jnp.concatenate([back_ref[d] for d in width_blocks], axis=1) * gain_ref[...]
    unit = unit_ref[...]
    dhidden = (
        dxhat
        - jnp.mean(dxhat, axis=1, keepdims=True)
        - unit * jnp.mean(dxhat * unit, axis=1, keepdims=True)
    )
    rstd = rstd_ref[:, 0:1]
    grad_out_ref[0] = (grad_ref[0].astype(jnp.float32) + rstd * dhidden).astype(jnp.bfloat16)


def mlp_far(table, gain, grad_out, state, firsts, seconds):
    near = len(firsts)
    shape = grad_out.shape
    kept = (table.shape[1] // 2, shape[1], BLK)
    args = (gain, grad_out, *state, *firsts, *seconds)
    return pl.pallas_call(
        functools.partial(far_kernel, near),
        out_shape=[jax.ShapeDtypeStruct(shape, jnp.bfloat16)] * 2,
        in_specs=[vmem()] * (1 + len(args)),
        out_specs=[vmem()] * 2,
        scratch_shapes=[pltpu.VMEM(state[0].shape, jnp.float32)] * 2
        + [pltpu.VMEM(kept, jnp.bfloat16)] * 2
        + [pltpu.SMEM(table.shape, jnp.int32), pltpu.SemaphoreType.DMA],
        compiler_params=pltpu.CompilerParams(vmem_limit_bytes=VMEM_LIMIT),
        name="mlp_far",
    )(table, *args)


def body(
    seq_size,
    grp_size,
    tokens,
    queries,
    keys,
    values,
    attn_mask,
    out_proj,
    norm_gain_vector,
    w1_packed,
    w1_rows,
    w2_packed,
    w2_cols,
    grad_out,
):
    flips = [f for f in flips_of(seq_size) if f and f & (f - 1) == 0]
    across = grp_size // 2
    near_bits = []
    bit = across // 2
    while bit:
        near_bits.append(bit)
        bit //= 2

    def over_seq(x, flip):
        return exchange(x, "seq", seq_size, flip)

    def over_grp(x, flip):
        return exchange(x, "grp", grp_size, flip)

    masks = [0]
    for bit in near_bits:
        masks = masks + [m ^ bit for m in masks]
    order = sorted(range(len(masks)), key=lambda i: masks[i])

    def over_near(x):
        held = butterfly(x, "grp", grp_size, near_bits)
        return [held[i] for i in order]

    far_second = over_grp(w2_packed, across)
    far_first = over_grp(w1_packed, across)
    packed = pack(queries, keys, values, attn_mask, seq_size)
    packed = {0: packed[0], **{s: over_seq(packed[s], s * HEAD_BIT) for s in ORDER}}
    packed = [packed[s] for s in range(QUADS)]
    held = [butterfly(p[BLK : 3 * BLK], "seq", seq_size, flips) for p in packed]
    near_seconds = over_near(after(w2_packed, *packed[1:]))
    near_firsts = over_near(after(w1_packed, *packed[1:]))
    *state, table, gain = attend_own(packed, w1_rows, w2_cols, norm_gain_vector)
    rest = [held[u][t] for t in range(1, len(held[0])) for u in range(QUADS)]
    far_seconds = over_near(after(far_second, state[0]))
    attn = attend_rest(packed, rest, state)
    attn = {0: attn[0], **{s: over_seq(attn[s], s * HEAD_BIT) for s in ORDER}}
    attn = [attn[s] for s in range(QUADS)]
    far_firsts = over_near(after(far_first, *attn[1:]))
    state = mlp_near(
        table, attn, out_proj, tokens, gain, grad_out, near_firsts, near_seconds + far_seconds
    )
    output, grad_tokens = mlp_far(table, gain, grad_out, state, far_firsts, far_seconds)
    return (output, grad_tokens)


def solution(mesh):
    return jax.shard_map(
        functools.partial(body, mesh.shape["seq"], mesh.shape["grp"]),
        mesh=mesh,
        in_specs=(
            P("grp", "seq", None),
            P("grp", "seq", None),
            P("grp", "seq", None),
            P("grp", "seq", None),
            P("grp", "seq", None),
            P(),
            P(),
            P("grp", None, None, None),
            P(),
            P("grp", None, None, None),
            P(),
            P("grp", "seq", None),
        ),
        out_specs=(P("grp", "seq", None), P("grp", "seq", None)),
        check_vma=False,
    )
```
